256 devices in a mesh: group: 4 (over y_lo, core), dp: 8 (over x, y_hi), mp: 8 (over z).
Axes of the slice: x: 4, y: 4 (y_hi: 2, y_lo: 2; y = y_hi * 2 + y_lo), z: 8, core: 2. Of those that a mesh axis runs over, the one named last changes fastest.
Arguments:
- latent_noise: bfloat16 [16, 256, 1280], P('dp'), may hold values from -6 to 6
- score_noise: bfloat16 [16, 256, 1280], P('dp'), may hold values from -6 to 6
- timesteps: int32 [16], P('dp'), may hold values from 20 to 979
- classes: int32 [16], P('dp'), may hold values from 0 to 999
- class_table: bfloat16 [1000, 1280], replicated, may hold values from -6 to 6
- gen_weights: bfloat16 [1280, 2, 5120], P(('group', 'dp'), None, 'mp'), may hold values from -0.15625 to 0.15625
- real_weights: bfloat16 [1280, 2, 5120], P(('group', 'dp'), None, 'mp'), may hold values from -0.15625 to 0.15625
- fake_weights: bfloat16 [1280, 2, 5120], P(('group', 'dp'), None, 'mp'), may hold values from -0.15625 to 0.15625
Outputs:
- gen_grad: float32 [1280, 2, 5120], P(('group', 'dp'), None, 'mp')
- fake_grad: float32 [1280, 2, 5120], P(('group', 'dp'), None, 'mp')
The draws below stay inside these ranges and needn't reach their ends.
All inputs are finite; a program needn't handle non-finite values. Where the reference program divides by a largest or mean magnitude, that divisor is 1e-20 or more.
Results may differ from the reference program's by a relative error of at most 0.015.
Values may be sent and summed in bfloat16 or wider, within the bound.
No kernel may reach another device: no remote copies, remote signals or barrier semaphores. Data moves between devices by JAX's collectives and lax.ppermute only.
A program may use at most 128 MiB of HBM per device.

```python
import math
import jax
import jax.numpy as jnp
import numpy as np
from jax import lax

C = 1280
FF = 5120
CLASSES = 1000
HW = 256
TSTEPS = 1000
SAMPLES = 16
N_MP = 8


def touch_ends(array, key, smallest, largest):
    index_at = [jax.random.randint(jax.random.fold_in(key, axis), (), 0, length) for axis, length in enumerate(array.shape)]
    main_axis = array.shape.index(max(array.shape))
    neighbour = index_at[:main_axis] + [(index_at[main_axis] + 1) % array.shape[main_axis]] + index_at[main_axis + 1:]
    return array.at[tuple(index_at)].set(smallest).at[tuple(neighbour)].set(largest)


def levels(key, dims, shards, smallest, high):
    def one(dim, parts):
        draws = jax.random.uniform(jax.random.fold_in(jax.random.fold_in(key, 6), dim), (parts,), jnp.float32, smallest / len(shards), high / len(shards))
        return jnp.repeat(jnp.exp(draws), dims[dim] // parts).reshape((-1,) + (1,) * (len(dims) - dim - 1))

    loudness = one(*shards[0])
    for cut in shards[1:]:
        loudness = loudness * one(*cut)
    return loudness


def cumulative_ranks(count, skew):
    weights = [(1 << 20) // math.isqrt(grade ** skew) + 1 for grade in range(1, count + 1)]
    spread = 1 + sum(weights) // (1 << 30)
    return np.cumsum(np.array([max(1, weight // spread) for weight in weights]))


def ranked(stream_key, dims, count, skew):
    listing = cumulative_ranks(count, skew)
    pick = jax.random.randint(jax.random.fold_in(stream_key, 1), dims, 0, int(listing[count - 1]))
    standing = jnp.searchsorted(jnp.asarray(listing, jnp.int32), pick, side="right")
    return jax.random.permutation(jax.random.fold_in(stream_key, 2), count)[standing].astype(jnp.int32)


def gaussian(rng, shape, width, reach, cuts=(), kind=jnp.bfloat16):
    level = levels(rng, shape, cuts, -0.22, 0.18) if cuts else 1.0
    drawn = jax.random.normal(rng, shape, jnp.float32) * width * level
    return jnp.minimum(jnp.maximum(drawn, -reach), reach).astype(kind)


def setup_inputs(seed: int = 0) -> dict:
    key_of = jax.random.split(jax.random.key(seed), 9)
    return {
        "latent_noise": gaussian(key_of[0], (SAMPLES, HW, C), 1.0, 6.0, ((0, 8),)),
        "score_noise": gaussian(key_of[1], (SAMPLES, HW, C), 1.0, 6.0, ((0, 8),)),
        "timesteps": touch_ends(jax.random.randint(key_of[2], (SAMPLES,), 20, TSTEPS - 20), jax.random.fold_in(key_of[2], 1), 20, (TSTEPS - 20) - 1).astype(jnp.int32),
        "classes": touch_ends(ranked(key_of[3], (SAMPLES,), CLASSES, 2), jax.random.fold_in(key_of[3], 3), 0, CLASSES - 1).astype(jnp.int32),
        "class_table": gaussian(key_of[4], (CLASSES, C), 1.0, 6.0),
        "gen_weights": gaussian(key_of[5], (C, 2, FF), C ** -0.5, 0.15625, ((0, 32), (2, 8))),
        "real_weights": gaussian(key_of[6], (C, 2, FF), C ** -0.5, 0.15625, ((0, 32), (2, 8))),
        "fake_weights": gaussian(key_of[7], (C, 2, FF), C ** -0.5, 0.15625, ((0, 32), (2, 8))),
    }


GUIDANCE = 3.0
EPSILON = 1e-06
MEAN_EPS = 1e-05

def normalize(stream_in, embedding):
    summed = stream_in.astype(jnp.float32) + embedding.astype(jnp.float32)[:, None, :]
    factor = lax.rsqrt(lax.optimization_barrier(jnp.mean(summed * summed, axis=-1, keepdims=True)) + EPSILON)
    return (summed * factor).astype(jnp.bfloat16).reshape(-1, summed.shape[-1])

def network(stream_in, embedding, weights):
    normed = normalize(stream_in, embedding)
    w_in = weights[:, 0, :]
    w_out = weights[:, 1, :]
    preact = jnp.dot(normed, w_in, preferred_element_type=jnp.float32)
    active = jax.nn.gelu(preact).astype(jnp.bfloat16)
    shard_width = FF // N_MP
    total = jnp.zeros((normed.shape[0], C), jnp.float32)
    for shard in range(N_MP):
        part_act = active[:, shard * shard_width:(shard + 1) * shard_width]
        part_w = w_out[:, shard * shard_width:(shard + 1) * shard_width]
        partial_sum = lax.dot_general(part_act, part_w, (((1,), (1,)), ((), ())), preferred_element_type=jnp.float32)
        total = total + lax.optimization_barrier(partial_sum.astype(jnp.bfloat16)).astype(jnp.float32)
    output = stream_in.reshape(-1, C).astype(jnp.float32) + total
    return (output, normed, preact, active)

def weight_grads(normed, preact, active, w_out, delta):
    out_part = lax.dot_general(delta, active, (((0,), (0,)), ((), ())), preferred_element_type=jnp.float32)
    back = jnp.dot(delta, w_out, preferred_element_type=jnp.float32)
    unused, pull = jax.vjp(jax.nn.gelu, preact)
    pre_delta = pull(back)[0].astype(jnp.bfloat16)
    in_part = lax.dot_general(normed, pre_delta, (((0,), (0,)), ((), ())), preferred_element_type=jnp.float32)
    return jnp.stack([in_part, out_part], axis=1)

def reference(latent_noise, score_noise, timesteps, classes, class_table, gen_weights, real_weights, fake_weights):
    onehot = (classes[:, None] == jnp.arange(CLASSES, dtype=jnp.int32)[None, :]).astype(jnp.bfloat16)
    embedding = jnp.dot(onehot, class_table, preferred_element_type=jnp.float32).astype(jnp.bfloat16)
    latents, gen_normed, gen_preact, gen_active = network(latent_noise, embedding, gen_weights)
    phase_angle = 0.5 * jnp.pi / TSTEPS * timesteps.astype(jnp.float32)
    signal_scale = jnp.cos(phase_angle)[:, None, None]
    noise_scale = jnp.sin(phase_angle)[:, None, None]
    stream_lat = latents.reshape(SAMPLES, HW, C)
    noised = (signal_scale * stream_lat + noise_scale * score_noise.astype(jnp.float32)).astype(jnp.bfloat16)
    real_uncond = network(noised, jnp.zeros_like(embedding), real_weights)[0]
    real_cond = network(noised, embedding, real_weights)[0]
    fake_pred, fake_normed, fake_preact, fake_active = network(noised, embedding, fake_weights)
    real_mix = real_uncond + GUIDANCE * (real_cond - real_uncond)
    lat_f = latents
    fake_f = fake_pred
    gap = lax.optimization_barrier(jnp.mean(jnp.abs(lat_f - real_mix).reshape(SAMPLES, HW * C), axis=1))
    sample_weight = 1.0 / (gap + MEAN_EPS)
    row_weight = jnp.repeat(sample_weight, HW)[:, None]
    loss_scale = 1.0 / jnp.sqrt(jnp.float32(SAMPLES * HW))
    gen_delta = ((fake_f - real_mix) * row_weight * loss_scale).astype(jnp.bfloat16)
    fake_delta = (2.0 * (fake_f - lat_f) * loss_scale).astype(jnp.bfloat16)
    gen_grad = weight_grads(gen_normed, gen_preact, gen_active, gen_weights[:, 1, :], gen_delta)
    fake_grad = weight_grads(fake_normed, fake_preact, fake_active, fake_weights[:, 1, :], fake_delta)
    return (gen_grad, fake_grad)
```

```python
import math

import jax
import jax.numpy as jnp
from jax import lax
from jax.experimental import pallas as pl
from jax.experimental.pallas import tpu as pltpu
from jax.sharding import PartitionSpec as P

TSTEPS = 1000
GUIDANCE = 3.0
EPSILON = 1e-06
MEAN_EPS = 1e-05

PLANE = ("group", "dp")
LANES = 128
SMEM = pl.BlockSpec(memory_space=pltpu.SMEM)
VMEM = pl.BlockSpec(memory_space=pltpu.VMEM)
F32 = jnp.float32
BF16 = jnp.bfloat16


def call(body, name, inputs, scalars, outs, flops=0, scratch=()):
    moved = sum(math.prod(a.shape) * a.dtype.itemsize for a in list(inputs) + list(outs))
    return pl.pallas_call(
        body,
        name=name,
        out_shape=outs,
        in_specs=[SMEM] * len(scalars) + [VMEM] * len(inputs),
        out_specs=[VMEM] * len(outs),
        scratch_shapes=list(scratch),
        compiler_params=pltpu.CompilerParams(vmem_limit_bytes=40 * 2**20),
        cost_estimate=pl.CostEstimate(flops=flops, bytes_accessed=moved, transcendentals=0),
    )(*scalars, *inputs)


def shape(dims, dtype):
    return jax.ShapeDtypeStruct(dims, dtype)


def normalize(summed):
    factor = lax.rsqrt(jnp.mean(summed * summed, axis=-1, keepdims=True) + EPSILON)
    return (summed * factor).astype(BF16)


def dot_t(left, right):
    return lax.dot_general(left, right, (((1,), (1,)), ((), ())), preferred_element_type=F32)


def forward_part(normed, w_in, w_out):
    preact = jnp.dot(normed, w_in, preferred_element_type=F32)
    active = jax.nn.gelu(preact).astype(BF16)
    return preact, active, dot_t(active, w_out).astype(BF16)


def core_swap(block):
    return lax.ppermute(block, "group", [(0, 1), (1, 0), (2, 3), (3, 2)])


def shift(block, step):
    n_mp = lax.axis_size("mp")
    return lax.ppermute(block, "mp", [(i, (i + step) % n_mp) for i in range(n_mp)])


def spread(block):
    return [block] + [shift(block, k) for k in range(1, lax.axis_size("mp"))]


def to_owner(blocks):
    return [blocks[0]] + [shift(blocks[k], -k) for k in range(1, len(blocks))]


def on_core(place, run, mine, other):
    pl.when(place[0] == 0)(lambda: run(mine, other))
    pl.when(place[0] != 0)(lambda: run(other, mine))


def power_of(peak):
    return jnp.floor(jnp.log(jnp.maximum(peak, 1e-30)) * (1.0 / math.log(2.0))) - 13.0


def top_of(value):
    by_row = jnp.max(jnp.abs(value), axis=1, keepdims=True)
    return jnp.max(by_row, axis=0, keepdims=True)


def ring_place(place, k, piece, n_mp):
    return pl.multiple_of(lax.rem(place[2] + n_mp - k, n_mp) * piece, piece)


def prepare_kernel(place, scales, latent, noise, embed, normed, stream, scaled, *, piece, n_mp):
    base = pl.multiple_of(place[0] * (piece * n_mp), piece)
    rows = latent[place[1], pl.ds(base, piece * n_mp), :].astype(F32)
    normed[...] = normalize(rows + embed[...])
    at = pl.multiple_of(base + place[2] * piece, piece)
    stream[...] = latent[place[1], pl.ds(at, piece), :].astype(F32)
    scaled[...] = scales[1] * noise[place[1], pl.ds(at, piece), :].astype(F32)


def gen_kernel(place, normed, mine, other, *refs, piece):
    preact_ref, active_ref, parts, whole = refs[0], refs[1], refs[2:-1], refs[-1]

    def run(w_in, w_out):
        preact, active, partial = forward_part(normed[...], w_in[...], w_out[...])
        preact_ref[...] = preact
        active_ref[...] = active
        whole[...] = partial

    on_core(place, run, mine, other)
    for k, part in enumerate(parts):
        part[...] = whole[pl.ds(ring_place(place, k, piece, len(parts)), piece), :]


def score_kernel(place, *refs, piece, n_mp, hidden):
    blocks, refs = refs[:n_mp], refs[n_mp:]
    embed, score_mine, score_other, normed_ref, preact_ref, active_ref, out, both = refs
    rows = piece * n_mp
    width = embed.shape[1]
    for k, block in enumerate(blocks):
        summed = block[...].astype(F32)
        at = ring_place(place, k, piece, n_mp)
        both[pl.ds(at, piece), :] = normalize(summed + embed[...])
        both[pl.ds(pl.multiple_of(rows + at, piece), piece), :] = normalize(summed)
    normed_ref[...] = both[:rows, :]

    def run(mine, other):
        preact, active, fake = forward_part(both[:rows, :], mine[:, :hidden], other[:, :hidden])
        preact_ref[...] = preact
        active_ref[...] = active
        fake = fake.astype(F32)
        real = forward_part(both[...], mine[:, hidden:], other[:, hidden:])[2].astype(F32)
        uncond, cond = real[rows:], real[:rows]
        mix = uncond + GUIDANCE * (cond - uncond)
        fake_power, mix_power = power_of(top_of(fake)), power_of(top_of(mix))
        fake = fake * jnp.exp2(-fake_power)
        mix = mix * jnp.exp2(-mix_power)
        line = lax.broadcasted_iota(jnp.int32, (piece, LANES), 0)
        tail = jnp.where(line < 8, fake_power, mix_power)
        for j in range(n_mp):
            out[j, :, :width] = fake[j * piece : (j + 1) * piece, :]
            out[j, :, width : 2 * width] = mix[j * piece : (j + 1) * piece, :]
            out[j, :, 2 * width :] = tail

    on_core(place, run, score_mine, score_other)


def mix_kernel(blocks, latents, noised, fake_delta, gap_ref, apart, *, n_mp, loss_scale):
    base = noised[...].astype(F32)
    width = base.shape[1]
    fake = real = 0.0
    for j in range(n_mp):
        tail = blocks[j, :, 2 * width :]
        fake = fake + blocks[j, :, :width] * jnp.exp2(tail[0:1, 0:1])
        real = real + blocks[j, :, width : 2 * width] * jnp.exp2(tail[8:9, 0:1])
    fake = base + fake
    real_mix = base + real
    fake_delta[...] = (2.0 * (fake - latents[...]) * loss_scale).astype(BF16)
    apart[...] = fake - real_mix
    away = jnp.sum(jnp.abs(latents[...] - real_mix), axis=1, keepdims=True)
    gap_ref[...] = jnp.broadcast_to(jnp.sum(away, axis=0, keepdims=True), gap_ref.shape)


def pack_kernel(fake_delta, apart, gap_own, gap_other, out):
    width = apart.shape[1]
    fake = fake_delta[...].astype(F32)
    fake_power, apart_power = power_of(top_of(fake)), power_of(top_of(apart[...]))
    out[:, :width] = fake * jnp.exp2(-fake_power)
    out[:, width : 2 * width] = apart[...] * jnp.exp2(-apart_power)
    gap = gap_own[0:1, 0:1] + gap_other[0:1, 0:1]
    gap_power = power_of(gap)
    scaled = gap * jnp.exp2(-gap_power)
    high = jnp.floor(scaled * (1.0 / 16.0)) * 16.0
    line = lax.broadcasted_iota(jnp.int32, (fake.shape[0], LANES), 0)
    tail = jnp.where(line < 4, fake_power, apart_power)
    tail = jnp.where(line == 8, gap_power, tail)
    tail = jnp.where(line == 9, high, tail)
    out[:, 2 * width :] = jnp.where(line == 10, scaled - high, tail)


def back_kernel(place, blocks, *refs, n_mp, loss_scale, count, hidden):
    score_mine, score_other, gen_mine, gen_other = refs[:4]
    slopes, normed, active = refs[4:6], refs[6:8], refs[8:10]
    left, right, away = refs[10:]
    width = normed[0].shape[1]
    piece = blocks.shape[1]
    gap = 0.0
    for j in range(n_mp):
        tail = blocks[j, :, 2 * width :]
        gap = gap + (tail[9:10, 0:1] + tail[10:11, 0:1]) * jnp.exp2(tail[8:9, 0:1])
    weight = 1.0 / (gap / count + MEAN_EPS)
    for j in range(n_mp):
        tail = blocks[j, :, 2 * width :]
        fake = blocks[j, :, :width] * jnp.exp2(tail[0:1, 0:1])
        apart = blocks[j, :, width : 2 * width] * jnp.exp2(tail[4:5, 0:1])
        left[0, j * piece : (j + 1) * piece, :] = fake.astype(BF16)
        left[1, j * piece : (j + 1) * piece, :] = (apart * weight * loss_scale).astype(BF16)

    def run(score_out, gen_out):
        back = jnp.dot(left[0], score_out[:, :hidden], preferred_element_type=F32)
        right[0] = (back * slopes[0][...]).astype(BF16)
        back = jnp.dot(left[1], gen_out[...], preferred_element_type=F32)
        right[1] = (back * slopes[1][...]).astype(BF16)

    @pl.when(place[0] == 0)
    def _():
        run(score_other, gen_other)
        for m in range(2):
            away[m, :, :width] = left[m]
            away[m, :, width:] = active[m][...]
            left[m] = normed[m][...]

    @pl.when(place[0] != 0)
    def _():
        run(score_mine, gen_mine)
        for m in range(2):
            away[m, :, :width] = normed[m][...]
            away[m, :, width:] = right[m]
            right[m] = active[m][...]


def grad_kernel(left, right, came, out, both, grads, *, width, row_piece):
    rows = left.shape[1]
    size = (out.shape[1] - 16) // 2
    chunk = row_piece * 8
    powers = []
    for m in range(2):
        both[:rows, :width] = left[m]
        both[:rows, width:] = right[m]
        both[rows:, :] = came[m]
        turned = both[:, :width].T
        highest = jnp.zeros((8, LANES), F32)
        for c in range(width // chunk):
            block = jnp.dot(
                turned[c * chunk : (c + 1) * chunk, :], both[:, width:], preferred_element_type=F32
            )
            grads[c * chunk : (c + 1) * chunk, :] = block
            for t in range(block.shape[1] // LANES):
                lanes = jnp.abs(block[:, t * LANES : (t + 1) * LANES]).reshape(-1, 8, LANES)
                highest = jnp.maximum(highest, jnp.max(lanes, axis=0))
        power = power_of(top_of(highest))
        factor = jnp.exp2(-power)
        for d in range(width // row_piece):
            for t in range(grads.shape[1] // LANES):
                out[d, m * size + t * row_piece : m * size + (t + 1) * row_piece, :] = (
                    grads[d * row_piece : (d + 1) * row_piece, t * LANES : (t + 1) * LANES] * factor
                )
        powers.append(power)
    line = lax.broadcasted_iota(jnp.int32, (16, LANES), 0)
    tail = jnp.where(line < 8, powers[0], powers[1])
    for d in range(width // row_piece):
        out[d, 2 * size :, :] = tail


def local(
    latent_noise,
    score_noise,
    timesteps,
    classes,
    class_table,
    gen_weights,
    real_weights,
    fake_weights,
):
    group_index = lax.axis_index("group")
    core = group_index % 2
    y_lo = group_index // 2
    n_dp = lax.axis_size("dp")
    n_mp = lax.axis_size("mp")
    samples, positions, width = latent_noise.shape
    rows = positions // 2
    piece = rows // n_mp
    row_piece, _, hidden = gen_weights.shape
    loss_scale = 1.0 / math.sqrt(samples * n_dp * positions)
    place = jnp.stack([core, y_lo, lax.axis_index("mp")]).astype(jnp.int32)
    work = 2 * rows * width * hidden

    def outgoing(models):
        side = jnp.concatenate(models, axis=2)
        part_in = jnp.broadcast_to(side[None, :, 0], (n_dp,) + side[:, 0].shape)
        part_out = jnp.broadcast_to(side[None, :, 1], (n_dp,) + side[:, 1].shape)
        return jnp.concatenate([part_in, part_out, part_in, part_out], axis=0)

    def gather(blocks):
        return lax.all_to_all(blocks, PLANE, 0, 0, tiled=True).reshape(width, -1)

    own_class = lax.dynamic_index_in_dim(classes, y_lo, keepdims=False)
    embedding = lax.dynamic_index_in_dim(class_table, own_class, keepdims=True).astype(F32)
    own_step = lax.dynamic_index_in_dim(timesteps, y_lo, keepdims=False)
    phase_angle = 0.5 * jnp.pi / TSTEPS * own_step.astype(F32)
    signal_scale = jnp.cos(phase_angle)
    scales = jnp.stack([signal_scale, jnp.sin(phase_angle)])
    prepared = call(
        lambda *refs: prepare_kernel(*refs, piece=piece, n_mp=n_mp),
        "prepare",
        [latent_noise, score_noise, embedding],
        [place, scales],
        [shape((rows, width), BF16), shape((piece, width), F32), shape((piece, width), F32)],
    )

    gen_mine, score_blocks, prepared, embedding, signal_scale = lax.optimization_barrier(
        (
            gather(outgoing([gen_weights])),
            outgoing([fake_weights, real_weights]),
            prepared,
            embedding,
            signal_scale,
        )
    )
    normed_gen, stream, scaled_noise = prepared
    score_mine = gather(score_blocks)
    gen_other = core_swap(gen_mine)

    preact_gen, active_gen, *parts = call(
        lambda *refs: gen_kernel(*refs, piece=piece),
        "generate",
        [normed_gen, gen_mine, gen_other],
        [place],
        [shape((rows, hidden), F32), shape((rows, hidden), BF16)]
        + [shape((piece, width), BF16)] * n_mp,
        2 * work,
        [pltpu.VMEM((rows, width), BF16)],
    )
    total = sum(block.astype(F32) for block in to_owner(parts))
    latents = stream + total
    noised = (signal_scale * latents + scaled_noise).astype(BF16)

    score_mine, _ = lax.optimization_barrier((score_mine, noised))
    score_other = core_swap(score_mine)
    normed_cond, preact_fake, active_fake, score_parts = call(
        lambda *refs: score_kernel(*refs, piece=piece, n_mp=n_mp, hidden=hidden),
        "score",
        spread(noised) + [embedding, score_mine, score_other],
        [place],
        [
            shape((rows, width), BF16),
            shape((rows, hidden), F32),
            shape((rows, hidden), BF16),
            shape((n_mp, piece, 2 * width + LANES), F32),
        ],
        6 * work,
        [pltpu.VMEM((2 * rows, width), BF16)],
    )

    def exchange(blocks):
        return lax.all_to_all(blocks.astype(jnp.float16), "mp", 0, 0, tiled=True).astype(F32)

    fake_delta, gap_own, apart = call(
        lambda *refs: mix_kernel(*refs, n_mp=n_mp, loss_scale=loss_scale),
        "mix",
        [exchange(score_parts), latents, noised],
        [],
        [shape((piece, width), BF16), shape((8, LANES), F32), shape((piece, width), F32)],
    )
    (message,) = call(
        pack_kernel,
        "pack",
        [fake_delta, apart, gap_own, core_swap(gap_own)],
        [],
        [shape((piece, 2 * width + LANES), F32)],
    )

    def slope_of(preact):
        return jax.vjp(jax.nn.gelu, preact)[1](jnp.ones_like(preact))[0]

    left, right, away = call(
        lambda *refs: back_kernel(
            *refs, n_mp=n_mp, loss_scale=loss_scale, count=positions * width, hidden=hidden
        ),
        "back",
        [
            exchange(jnp.broadcast_to(message[None], (n_mp,) + message.shape)),
            score_mine,
            score_other,
            gen_mine,
            gen_other,
            slope_of(preact_fake),
            slope_of(preact_gen),
            normed_cond,
            normed_gen,
            active_fake,
            active_gen,
        ],
        [place],
        [
            shape((2, rows, width), BF16),
            shape((2, rows, hidden), BF16),
            shape((2, rows, width + hidden), BF16),
        ],
        2 * work,
    )
    size = row_piece * hidden // LANES
    (grads,) = call(
        lambda *refs: grad_kernel(*refs, width=width, row_piece=row_piece),
        "outer",
        [left, right, core_swap(away)],
        [],
        [shape((width // row_piece, 2 * size + 16, LANES), F32)],
        4 * work,
        [pltpu.VMEM((2 * rows, width + hidden), BF16), pltpu.VMEM((width, hidden), F32)],
    )
    came = lax.all_to_all(grads.astype(jnp.float16), PLANE, 0, 0, tiled=True)

    def collect(index):
        factor = jnp.exp2(came[:, 2 * size + 8 * index, 0].astype(F32))[:, None, None]
        own = came[:, index * size : (index + 1) * size].astype(F32) * factor
        summed = jnp.sum(own.reshape(2, 2, n_dp, size, LANES), axis=(0, 2))
        summed = summed.reshape(2, hidden // LANES, row_piece, LANES)
        return summed.transpose(2, 0, 1, 3).reshape(row_piece, 2, hidden)

    return (collect(1), collect(0))


def solution(mesh):
    return jax.shard_map(
        local,
        mesh=mesh,
        in_specs=(
            P("dp", None, None),
            P("dp", None, None),
            P("dp"),
            P("dp"),
            P(),
            P(("group", "dp"), None, "mp"),
            P(("group", "dp"), None, "mp"),
            P(("group", "dp"), None, "mp"),
        ),
        out_specs=(P(("group", "dp"), None, "mp"), P(("group", "dp"), None, "mp")),
        check_vma=False,
    )
```

```python
import math

import jax
import jax.numpy as jnp
from jax import lax
from jax.experimental import pallas as pl
from jax.experimental.pallas import tpu as pltpu
from jax.sharding import PartitionSpec as P

TSTEPS = 1000
GUIDANCE = 3.0
EPSILON = 1e-06
MEAN_EPS = 1e-05

PLANE = ("group", "dp")
LANES = 128
WALK = [(0, 0), (1, 0), (2, 0), (3, 0), (3, 1), (2, 1), (1, 1), (1, 2)]
WALK += [(2, 2), (3, 2), (3, 3), (2, 3), (1, 3), (0, 3), (0, 2), (0, 1)]
SLOTS = [
    (WALK.index((x, y_hi * 2 + y_lo)), core)
    for y_lo in range(2)
    for core in range(2)
    for x in range(4)
    for y_hi in range(2)
]
PEERS = [[((y % 2) * 2 + core) * 8 + x * 2 + y // 2 for x, y in WALK] for core in range(2)]
SMEM = pl.BlockSpec(memory_space=pltpu.SMEM)
VMEM = pl.BlockSpec(memory_space=pltpu.VMEM)
F32 = jnp.float32
BF16 = jnp.bfloat16


def call(body, name, inputs, scalars, outs, flops=0, scratch=()):
    moved = sum(math.prod(a.shape) * a.dtype.itemsize for a in list(inputs) + list(outs))
    return pl.pallas_call(
        body,
        name=name,
        out_shape=outs,
        in_specs=[SMEM] * len(scalars) + [VMEM] * len(inputs),
        out_specs=[VMEM] * len(outs),
        scratch_shapes=list(scratch),
        compiler_params=pltpu.CompilerParams(vmem_limit_bytes=40 * 2**20),
        cost_estimate=pl.CostEstimate(flops=flops, bytes_accessed=moved, transcendentals=0),
    )(*scalars, *inputs)


def shape(dims, dtype):
    return jax.ShapeDtypeStruct(dims, dtype)


def normalize(summed):
    factor = lax.rsqrt(jnp.mean(summed * summed, axis=-1, keepdims=True) + EPSILON)
    return (summed * factor).astype(BF16)


def dot_t(left, right):
    return lax.dot_general(left, right, (((1,), (1,)), ((), ())), preferred_element_type=F32)


def forward_part(normed, w_in, w_out):
    preact = jnp.dot(normed, w_in, preferred_element_type=F32)
    active = jax.nn.gelu(preact).astype(BF16)
    return preact, active, dot_t(active, w_out).astype(BF16)


def core_swap(block):
    return lax.ppermute(block, "group", [(0, 1), (1, 0), (2, 3), (3, 2)])


def shift(block, step):
    n_mp = lax.axis_size("mp")
    return lax.ppermute(block, "mp", [(i, (i + step) % n_mp) for i in range(n_mp)])


def spread(block):
    return [block] + [shift(block, k) for k in range(1, lax.axis_size("mp"))]


def to_owner(blocks):
    return [blocks[0]] + [shift(blocks[k], -k) for k in range(1, len(blocks))]


def on_core(place, run, mine, other):
    pl.when(place[0] == 0)(lambda: run(mine, other))
    pl.when(place[0] != 0)(lambda: run(other, mine))


def power_of(peak):
    return jnp.floor(jnp.log(jnp.maximum(peak, 1e-30)) * (1.0 / math.log(2.0))) - 13.0


def top_of(value):
    by_row = jnp.max(jnp.abs(value), axis=1, keepdims=True)
    return jnp.max(by_row, axis=0, keepdims=True)


def ring_place(place, k, piece, n_mp):
    return pl.multiple_of(lax.rem(place[2] + n_mp - k, n_mp) * piece, piece)


def lay_kernel(*refs):
    models, out = refs[:-1], refs[-1]
    count = out.shape[0] // 4
    if len(models) == 1:
        wholes = [models[0][:, side, :] for side in range(2)]
    else:
        wholes = [jnp.concatenate([m[:, 0, :], m[:, 1, :]], axis=1) for m in models]
    for core, whole in enumerate(wholes):
        for d in range(count):
            out[core * count + d] = whole
            out[(2 + core) * count + d] = whole


def prepare_kernel(place, scales, latent, noise, embed, normed, stream, scaled, *, piece):
    rows = latent[place[1]].astype(F32)
    normed[...] = normalize(rows + embed[...])
    at = pl.multiple_of(place[0] * (rows.shape[0] // 2) + place[2] * piece, piece)
    stream[...] = latent[place[1], pl.ds(at, piece), :].astype(F32)
    scaled[...] = scales[1] * noise[place[1], pl.ds(at, piece), :].astype(F32)


def gen_kernel(place, normed, mine, other, *refs, piece):
    preact_ref, active_ref, parts, whole = refs[0], refs[1], refs[2:-1], refs[-1]
    rows = whole.shape[0]
    own = normed[pl.ds(pl.multiple_of(place[0] * rows, rows), rows), :]

    def run(w_in, w_out):
        preact, active, partial = forward_part(own, w_in[...], w_out[...])
        preact_ref[...] = preact
        active_ref[...] = active
        whole[...] = partial

    on_core(place, run, mine, other)
    for k, part in enumerate(parts):
        part[...] = whole[pl.ds(ring_place(place, k, piece, len(parts)), piece), :]


def order_kernel(place, *refs):
    blocks, out = refs[:-1], refs[-1]
    piece = blocks[0].shape[0]
    for k, block in enumerate(blocks):
        out[pl.ds(ring_place(place, k, piece, len(blocks)), piece), :] = block[...]


def score_kernel(place, own, came, embed, weights, normed, preact_ref, active_ref, out, both):
    half, width = own.shape
    rows = 2 * half
    n_mp, piece = out.shape[0], out.shape[1] // 2
    hidden = weights.shape[1] // 2
    for source, core in ((own, place[0]), (came, 1 - place[0])):
        at = pl.multiple_of(core * half, half)
        summed = source[...].astype(F32)
        both[pl.ds(at, half), :] = normalize(summed + embed[...])
        both[pl.ds(pl.multiple_of(rows + at, half), half), :] = normalize(summed)
    normed[...] = both[:rows, :]

    def finish(value):
        power = power_of(top_of(value))
        value = value * jnp.exp2(-power)
        tail = jnp.broadcast_to(power, (2 * piece, LANES))
        for j in range(n_mp):
            for h in range(2):
                at = h * half + j * piece
                out[j, h * piece : (h + 1) * piece, :width] = value[at : at + piece, :]
            out[j, :, width:] = tail

    @pl.when(place[0] == 0)
    def _():
        preact, active, fake = forward_part(both[:rows, :], weights[:, :hidden], weights[:, hidden:])
        preact_ref[...] = preact
        active_ref[...] = active
        finish(fake.astype(F32))

    @pl.when(place[0] != 0)
    def _():
        preact, active, real = forward_part(both[...], weights[:, :hidden], weights[:, hidden:])
        preact_ref[...] = preact[:rows]
        active_ref[...] = active[:rows]
        uncond, cond = real[rows:].astype(F32), real[:rows].astype(F32)
        finish(uncond + GUIDANCE * (cond - uncond))


def total_kernel(blocks, out):
    width = out.shape[1]
    total = 0.0
    for j in range(blocks.shape[0]):
        total = total + blocks[j, :, :width] * jnp.exp2(blocks[j, 0:1, width : width + 1])
    out[...] = total


def pack_kernel(place, own, other, near, far, out, *, loss_scale):
    width = own.shape[1]
    piece = near.shape[1]
    first = place[0] == 0

    def run(fake_sum, real_sum, low, high):
        latents = jnp.concatenate([low[0], high[0]], axis=0)
        base = jnp.concatenate([low[1], high[1]], axis=0)
        fake = base + fake_sum[...]
        real_mix = base + real_sum[...]
        away = jnp.sum(jnp.abs(latents - real_mix), axis=1, keepdims=True)
        gap = jnp.sum(away, axis=0, keepdims=True)
        fake_delta = (2.0 * (fake - latents) * loss_scale).astype(BF16).astype(F32)
        value = jnp.where(first, fake_delta, fake - real_mix)
        power = power_of(top_of(value))
        out[:, :width] = value * jnp.exp2(-power)
        gap_power = power_of(gap)
        scaled = gap * jnp.exp2(-gap_power)
        coarse = jnp.floor(scaled * (1.0 / 16.0)) * 16.0
        line = lax.broadcasted_iota(jnp.int32, (2 * piece, LANES), 0)
        tail = jnp.where(line == 8, gap_power, power)
        tail = jnp.where(line == 9, coarse, tail)
        out[:, width:] = jnp.where(line == 10, scaled - coarse, tail)

    pl.when(first)(lambda: run(own, other, near, far))
    pl.when(place[0] != 0)(lambda: run(other, own, far, near))


def grad_kernel(
    place, blocks, weights, slope, normed, active, out, delta, grads, *, loss_scale, count, row_piece
):
    n_mp, piece = blocks.shape[0], blocks.shape[1] // 2
    rows, width = normed.shape
    hidden = active.shape[1]
    half = rows // 2
    gap = 0.0
    for j in range(n_mp):
        tail = blocks[j, :, width:]
        gap = gap + (tail[9:10, 0:1] + tail[10:11, 0:1]) * jnp.exp2(tail[8:9, 0:1])
    first = place[0] == 0
    weight = jnp.where(first, 1.0, 1.0 / (gap / count + MEAN_EPS))
    scale = jnp.where(first, 1.0, loss_scale)
    for j in range(n_mp):
        value = blocks[j, :, :width] * jnp.exp2(blocks[j, 0:1, width : width + 1])
        value = (value * weight * scale).astype(BF16)
        for h in range(2):
            at = h * half + j * piece
            delta[at : at + piece, :] = value[h * piece : (h + 1) * piece, :]
    size = row_piece * hidden // LANES
    chunk = row_piece * 8
    turned = delta[...].T
    powers = []

    def outer(side, turned, right):
        highest = jnp.zeros((8, LANES), F32)
        for c in range(width // chunk):
            block = jnp.dot(
                turned[c * chunk : (c + 1) * chunk, :], right, preferred_element_type=F32
            )
            grads[c * chunk : (c + 1) * chunk, :] = block
            for t in range(hidden // LANES):
                lanes = jnp.abs(block[:, t * LANES : (t + 1) * LANES]).reshape(-1, 8, LANES)
                highest = jnp.maximum(highest, jnp.max(lanes, axis=0))
        power = power_of(top_of(highest))
        factor = jnp.exp2(-power)
        for owner, (slot, part) in enumerate(SLOTS):
            for t in range(hidden // LANES):
                to = (part * 2 + side) * size + t * row_piece
                out[slot, to : to + row_piece, :] = (
                    grads[
                        owner * row_piece : (owner + 1) * row_piece,
                        t * LANES : (t + 1) * LANES,
                    ]
                    * factor
                )
        powers.append(power)

    outer(1, turned, active[...])
    back = jnp.dot(delta[...], weights[...], preferred_element_type=F32)
    outer(0, normed[...].T, (back * slope[...]).astype(BF16))
    line = lax.broadcasted_iota(jnp.int32, (16, LANES), 0)
    tail = jnp.where(line < 8, powers[1], powers[0])
    for d in range(out.shape[0]):
        out[d, 4 * size :, :] = tail


def collect_kernel(place, came, own, away):
    sources = came.shape[0]
    size = (came.shape[1] - 16) // 4
    for side in range(2):
        factors = [
            jnp.exp2(came[i, 4 * size + 8 * side : 4 * size + 8 * side + 1, 0:1])
            for i in range(sources)
        ]
        for out, core in ((own, place[0]), (away, 1 - place[0])):
            at = pl.multiple_of((core * 2 + side) * size, 8)
            total = came[0, pl.ds(at, size), :] * factors[0]
            for i in range(1, sources):
                total = total + came[i, pl.ds(at, size), :] * factors[i]
            out[side * size : (side + 1) * size, :] = total


def place_kernel(place, own, came, *outs):
    rows = outs[0].shape[0]
    tiles = outs[0].shape[2] // LANES

    def run(sources):
        for out, ref in zip(outs, sources):
            for side in range(2):
                for t in range(tiles):
                    at = (side * tiles + t) * rows
                    out[:, side, t * LANES : (t + 1) * LANES] = ref[at : at + rows, :]

    pl.when(place[0] == 0)(lambda: run((own, came)))
    pl.when(place[0] != 0)(lambda: run((came, own)))


def local(
    latent_noise,
    score_noise,
    timesteps,
    classes,
    class_table,
    gen_weights,
    real_weights,
    fake_weights,
):
    group_index = lax.axis_index("group")
    core = group_index % 2
    y_lo = group_index // 2
    n_dp = lax.axis_size("dp")
    n_mp = lax.axis_size("mp")
    samples, positions, width = latent_noise.shape
    rows = positions // 2
    piece = rows // n_mp
    row_piece, _, hidden = gen_weights.shape
    loss_scale = 1.0 / math.sqrt(samples * n_dp * positions)
    place = jnp.stack([core, y_lo, lax.axis_index("mp")]).astype(jnp.int32)
    work = 2 * rows * width * hidden

    def outgoing(models):
        lanes = hidden * len(models)
        return call(
            lay_kernel, "lay", models, [], [shape((4 * n_dp, row_piece, lanes), BF16)]
        )[0]

    def gather(blocks):
        return lax.all_to_all(blocks, PLANE, 0, 0, tiled=True).reshape(width, -1)

    own_class = lax.dynamic_index_in_dim(classes, y_lo, keepdims=False)
    embedding = lax.dynamic_index_in_dim(class_table, own_class, keepdims=True).astype(F32)
    own_step = lax.dynamic_index_in_dim(timesteps, y_lo, keepdims=False)
    phase_angle = 0.5 * jnp.pi / TSTEPS * own_step.astype(F32)
    signal_scale = jnp.cos(phase_angle)
    scales = jnp.stack([signal_scale, jnp.sin(phase_angle)])
    prepared = call(
        lambda *refs: prepare_kernel(*refs, piece=piece),
        "prepare",
        [latent_noise, score_noise, embedding],
        [place, scales],
        [
            shape((positions, width), BF16),
            shape((piece, width), F32),
            shape((piece, width), F32),
        ],
    )

    gen_mine, score_blocks, prepared, embedding, signal_scale = lax.optimization_barrier(
        (
            gather(outgoing([gen_weights])),
            outgoing([fake_weights, real_weights]),
            prepared,
            embedding,
            signal_scale,
        )
    )
    normed_gen, stream, scaled_noise = prepared
    score_weights = gather(score_blocks)
    gen_other = core_swap(gen_mine)

    preact_gen, active_gen, *parts = call(
        lambda *refs: gen_kernel(*refs, piece=piece),
        "generate",
        [normed_gen, gen_mine, gen_other],
        [place],
        [shape((rows, hidden), F32), shape((rows, hidden), BF16)]
        + [shape((piece, width), BF16)] * n_mp,
        2 * work,
        [pltpu.VMEM((rows, width), BF16)],
    )
    total = sum(block.astype(F32) for block in to_owner(parts))
    latents = stream + total
    noised = (signal_scale * latents + scaled_noise).astype(BF16)

    (noised_own,) = call(
        order_kernel, "order", spread(noised), [place], [shape((rows, width), BF16)]
    )
    score_weights, noised_own = lax.optimization_barrier((score_weights, noised_own))
    near = jnp.stack([latents, noised.astype(F32)])
    normed_cond, preact_fake, active_fake, score_parts = call(
        score_kernel,
        "score",
        [noised_own, core_swap(noised_own), embedding, score_weights],
        [place],
        [
            shape((positions, width), BF16),
            shape((positions, hidden), F32),
            shape((positions, hidden), BF16),
            shape((n_mp, 2 * piece, width + LANES), F32),
        ],
        8 * work,
        [pltpu.VMEM((2 * positions, width), BF16)],
    )

    def exchange(blocks):
        return lax.all_to_all(blocks.astype(jnp.float16), "mp", 0, 0, tiled=True).astype(F32)

    (total,) = call(
        total_kernel, "total", [exchange(score_parts)], [], [shape((2 * piece, width), F32)]
    )
    (message,) = call(
        lambda *refs: pack_kernel(*refs, loss_scale=loss_scale),
        "pack",
        [total, core_swap(total), near, core_swap(near)],
        [place],
        [shape((2 * piece, width + LANES), F32)],
    )

    first = core == 0

    def chosen(fake_value, gen_value):
        gen_all = jnp.concatenate([core_swap(gen_value), gen_value], axis=0)
        return jnp.where(first, fake_value, gen_all)

    preact = chosen(preact_fake, preact_gen)
    slope = jax.vjp(jax.nn.gelu, preact)[1](jnp.ones_like(preact))[0]
    size = row_piece * hidden // LANES
    (grads,) = call(
        lambda *refs: grad_kernel(
            *refs, loss_scale=loss_scale, count=positions * width, row_piece=row_piece
        ),
        "grads",
        [
            exchange(jnp.broadcast_to(message[None], (n_mp,) + message.shape)),
            jnp.where(first, score_weights[:, hidden:], gen_mine),
            slope,
            jnp.where(first, normed_cond, normed_gen),
            chosen(active_fake, active_gen),
        ],
        [place],
        [shape((len(WALK), 4 * size + 16, LANES), F32)],
        6 * work,
        [pltpu.VMEM((positions, width), BF16), pltpu.VMEM((width, hidden), F32)],
    )
    came = lax.all_to_all(
        grads.astype(jnp.float16), PLANE, 0, 0, axis_index_groups=PEERS, tiled=True
    )
    own, away = call(
        collect_kernel,
        "collect",
        [came.astype(F32)],
        [place],
        [shape((2 * size, LANES), F32)] * 2,
    )
    fake_grad, gen_grad = call(
        place_kernel,
        "place",
        [own, core_swap(away)],
        [place],
        [shape((row_piece, 2, hidden), F32)] * 2,
    )
    return (gen_grad, fake_grad)


def solution(mesh):
    return jax.shard_map(
        local,
        mesh=mesh,
        in_specs=(
            P("dp", None, None),
            P("dp", None, None),
            P("dp"),
            P("dp"),
            P(),
            P(("group", "dp"), None, "mp"),
            P(("group", "dp"), None, "mp"),
            P(("group", "dp"), None, "mp"),
        ),
        out_specs=(P(("group", "dp"), None, "mp"), P(("group", "dp"), None, "mp")),
        check_vma=False,
    )
```

```python
import math

import jax
import jax.numpy as jnp
from jax import lax
from jax.experimental import pallas as pl
from jax.experimental.pallas import tpu as pltpu
from jax.sharding import PartitionSpec as P

TSTEPS = 1000
GUIDANCE = 3.0
EPSILON = 1e-06
MEAN_EPS = 1e-05

PLANE = ("group", "dp")
LANES = 128
WALK = [(0, 0), (1, 0), (2, 0), (3, 0), (3, 1), (2, 1), (1, 1), (1, 2)]
WALK += [(2, 2), (3, 2), (3, 3), (2, 3), (1, 3), (0, 3), (0, 2), (0, 1)]
SLOTS = [
    (WALK.index((x, y_hi * 2 + y_lo)), core)
    for y_lo in range(2)
    for core in range(2)
    for x in range(4)
    for y_hi in range(2)
]
PEERS = [[((y % 2) * 2 + core) * 8 + x * 2 + y // 2 for x, y in WALK] for core in range(2)]
SMEM = pl.BlockSpec(memory_space=pltpu.SMEM)
VMEM = pl.BlockSpec(memory_space=pltpu.VMEM)
F32 = jnp.float32
BF16 = jnp.bfloat16


def call(body, name, inputs, scalars, outs, flops=0, scratch=(), room=40):
    moved = sum(math.prod(a.shape) * a.dtype.itemsize for a in list(inputs) + list(outs))
    return pl.pallas_call(
        body,
        name=name,
        out_shape=outs,
        in_specs=[SMEM] * len(scalars) + [VMEM] * len(inputs),
        out_specs=[VMEM] * len(outs),
        scratch_shapes=list(scratch),
        compiler_params=pltpu.CompilerParams(vmem_limit_bytes=room * 2**20),
        cost_estimate=pl.CostEstimate(flops=flops, bytes_accessed=moved, transcendentals=0),
    )(*scalars, *inputs)


def shape(dims, dtype):
    return jax.ShapeDtypeStruct(dims, dtype)


def normalize(summed):
    factor = lax.rsqrt(jnp.mean(summed * summed, axis=-1, keepdims=True) + EPSILON)
    return (summed * factor).astype(BF16)


def dot_t(left, right):
    return lax.dot_general(left, right, (((1,), (1,)), ((), ())), preferred_element_type=F32)


def forward_part(normed, w_in, w_out):
    preact = jnp.dot(normed, w_in, preferred_element_type=F32)
    active = jax.nn.gelu(preact).astype(BF16)
    return preact, active, dot_t(active, w_out).astype(BF16)


def core_swap(block):
    return lax.ppermute(block, "group", [(0, 1), (1, 0), (2, 3), (3, 2)])


def paired(block, step):
    n_mp = lax.axis_size("mp")
    pairs = []
    for group in range(lax.axis_size("group")):
        sign = 1 - 2 * (group % 2)
        for z in range(n_mp):
            pairs.append((group * n_mp + z, group * n_mp + (z + sign * step) % n_mp))
    return lax.ppermute(block, ("group", "mp"), pairs)


def on_core(place, run, mine, other):
    pl.when(place[0] == 0)(lambda: run(mine, other))
    pl.when(place[0] != 0)(lambda: run(other, mine))


def power_of(peak):
    return jnp.floor(jnp.log(jnp.maximum(peak, 1e-30)) * (1.0 / math.log(2.0))) - 13.0


def top_of(value):
    by_row = jnp.max(jnp.abs(value), axis=1, keepdims=True)
    return jnp.max(by_row, axis=0, keepdims=True)


def above(place, core, step, n_mp):
    return lax.rem(place[2] + n_mp + (1 - 2 * core) * step, n_mp)


def row_at(index, size):
    return pl.multiple_of(index * size, size)


def lay_kernel(*refs):
    models, out = refs[:-1], refs[-1]
    count = out.shape[0] // 4
    if len(models) == 1:
        wholes = [models[0][:, side, :] for side in range(2)]
    else:
        wholes = [jnp.concatenate([m[:, 0, :], m[:, 1, :]], axis=1) for m in models]
    for core, whole in enumerate(wholes):
        for d in range(count):
            out[core * count + d] = whole
            out[(2 + core) * count + d] = whole


def prepare_kernel(place, scales, latent, noise, embed, normed, stream, scaled, *, piece):
    rows = latent[place[1]].astype(F32)
    normed[...] = normalize(rows + embed[...])
    half = rows.shape[0] // 2
    for core in range(2):
        at = pl.multiple_of(core * half + place[2] * piece, piece)
        to = slice(core * piece, (core + 1) * piece)
        stream[to, :] = latent[place[1], pl.ds(at, piece), :].astype(F32)
        scaled[to, :] = scales[1] * noise[place[1], pl.ds(at, piece), :].astype(F32)


def gen_kernel(place, normed, mine, other, preact_ref, active_ref, kept, across, own, away, whole):
    rows = whole.shape[0]
    piece = own.shape[0]
    n_mp = rows // piece
    core = place[0]
    rows_of = normed[pl.ds(row_at(core, rows), rows), :]

    def run(w_in, w_out):
        preact, active, partial = forward_part(rows_of, w_in[...], w_out[...])
        preact_ref[...] = preact
        active_ref[...] = active
        whole[...] = partial

    on_core(place, run, mine, other)
    own[...] = whole[pl.ds(row_at(place[2], piece), piece), :]
    across[...] = whole[pl.ds(row_at(above(place, core, n_mp // 2, n_mp), piece), piece), :]
    for k in range(1, n_mp // 2):
        to = slice((k - 1) * piece, k * piece)
        kept[to, :] = whole[pl.ds(row_at(above(place, core, k, n_mp), piece), piece), :]
        away[to, :] = whole[pl.ds(row_at(above(place, 1 - core, k, n_mp), piece), piece), :]


def join_kernel(kept, came, *outs):
    piece = outs[0].shape[0] // 2
    for k, out in enumerate(outs):
        out[:piece, :] = kept[k * piece : (k + 1) * piece, :]
        out[piece:, :] = came[k * piece : (k + 1) * piece, :]


def sums_kernel(own, across, *refs):
    blocks, out = refs[:-1], refs[-1]
    piece = own.shape[0]
    near = own[...].astype(F32) + across[...].astype(F32)
    far = 0.0
    for block in blocks:
        near = near + block[:piece, :].astype(F32)
        far = far + block[piece:, :].astype(F32)
    out[:piece, :] = near
    out[piece:, :] = far


def latent_kernel(place, scales, sums, came, stream, scaled, latents, noised, mine):
    piece = mine.shape[0]
    totals = (sums[:piece, :] + came[piece:, :], came[:piece, :] + sums[piece:, :])

    def run(ordered):
        for core, total in enumerate(ordered):
            at = slice(core * piece, (core + 1) * piece)
            latents[at, :] = stream[at, :] + total
            noised[at, :] = (scales[0] * latents[at, :] + scaled[at, :]).astype(BF16)

    pl.when(place[0] == 0)(lambda: run(totals))
    pl.when(place[0] != 0)(lambda: run(totals[::-1]))
    mine[...] = noised[pl.ds(row_at(place[0], piece), piece), :]


def order_kernel(*refs):
    blocks, out = refs[:-1], refs[-1]
    at = 0
    for block in blocks:
        out[at : at + block.shape[0], :] = block[...]
        at += block.shape[0]


def rows_in_order(place, own, came, pair, store):
    piece = pair.shape[0] // 2
    n_mp = (own.shape[0] // piece + 1) // 2 * 2
    half = n_mp * piece

    def at(core, z):
        return pl.multiple_of(core * half + z * piece, piece)

    for core in range(2):
        store(at(core, place[2]), pair[core * piece : (core + 1) * piece, :])
    for source, sender in ((own, place[0]), (came, 1 - place[0])):
        for k in range(1, n_mp // 2):
            z = above(place, sender, -k, n_mp)
            for core in range(2):
                to = ((k - 1) * 2 + core) * piece
                store(at(core, z), source[to : to + piece, :])
        to = (n_mp - 2) * piece
        store(at(sender, above(place, sender, n_mp // 2, n_mp)), source[to : to + piece, :])


def score_kernel(place, pair, own, came, embed, weights, out, both):
    n_mp, piece = out.shape[0], out.shape[1] // 2
    width = embed.shape[1]
    half = n_mp * piece
    rows = 2 * half
    hidden = weights.shape[1] // 2

    def store(at, value):
        summed = value.astype(F32)
        both[pl.ds(at, piece), :] = normalize(summed + embed[...])
        both[pl.ds(pl.multiple_of(rows + at, piece), piece), :] = normalize(summed)

    rows_in_order(place, own, came, pair, store)

    def finish(value):
        power = power_of(top_of(value))
        value = value * jnp.exp2(-power)
        tail = jnp.broadcast_to(power, (2 * piece, LANES))
        for j in range(n_mp):
            for h in range(2):
                at = h * half + j * piece
                out[j, h * piece : (h + 1) * piece, :width] = value[at : at + piece, :]
            out[j, :, width:] = tail

    @pl.when(place[0] == 0)
    def _():
        fake = forward_part(both[:rows, :], weights[:, :hidden], weights[:, hidden:])[2]
        finish(fake.astype(F32))

    @pl.when(place[0] != 0)
    def _():
        real = forward_part(both[...], weights[:, :hidden], weights[:, hidden:])[2]
        uncond, cond = real[rows:].astype(F32), real[:rows].astype(F32)
        finish(uncond + GUIDANCE * (cond - uncond))


def refresh_kernel(place, pair, own, came, embed, weights, normed, preact, active):
    def store(at, value):
        rows = value.shape[0]
        normed[pl.ds(at, rows), :] = normalize(value.astype(F32) + embed[...])

    rows_in_order(place, own, came, pair, store)
    hidden = preact.shape[1]
    preact[...] = jnp.dot(normed[...], weights[:, :hidden], preferred_element_type=F32)
    active[...] = jax.nn.gelu(preact[...]).astype(BF16)


def total_kernel(blocks, out):
    width = out.shape[1]
    total = 0.0
    for j in range(blocks.shape[0]):
        total = total + blocks[j, :, :width] * jnp.exp2(blocks[j, 0:1, width : width + 1])
    out[...] = total


def pack_kernel(place, own, other, latents_ref, noised, out, *, loss_scale):
    width = own.shape[1]
    piece = own.shape[0] // 2
    first = place[0] == 0

    def run(fake_sum, real_sum):
        latents = latents_ref[...]
        base = noised[...].astype(F32)
        fake = base + fake_sum[...]
        real_mix = base + real_sum[...]
        away = jnp.sum(jnp.abs(latents - real_mix), axis=1, keepdims=True)
        gap = jnp.sum(away, axis=0, keepdims=True)
        fake_delta = (2.0 * (fake - latents) * loss_scale).astype(BF16).astype(F32)
        value = jnp.where(first, fake_delta, fake - real_mix)
        power = power_of(top_of(value))
        out[:, :width] = value * jnp.exp2(-power)
        gap_power = power_of(gap)
        scaled = gap * jnp.exp2(-gap_power)
        coarse = jnp.floor(scaled * (1.0 / 16.0)) * 16.0
        line = lax.broadcasted_iota(jnp.int32, (2 * piece, LANES), 0)
        tail = jnp.where(line == 8, gap_power, power)
        tail = jnp.where(line == 9, coarse, tail)
        out[:, width:] = jnp.where(line == 10, scaled - coarse, tail)

    pl.when(first)(lambda: run(own, other))
    pl.when(place[0] != 0)(lambda: run(other, own))


def grad_kernel(
    place, blocks, weights, slope, normed, active, out, delta, grads, *, loss_scale, count, row_piece
):
    n_mp, piece = blocks.shape[0], blocks.shape[1] // 2
    rows, width = normed.shape
    hidden = active.shape[1]
    half = rows // 2
    gap = 0.0
    for j in range(n_mp):
        tail = blocks[j, :, width:]
        gap = gap + (tail[9:10, 0:1] + tail[10:11, 0:1]) * jnp.exp2(tail[8:9, 0:1])
    first = place[0] == 0
    weight = jnp.where(first, 1.0, 1.0 / (gap / count + MEAN_EPS))
    scale = jnp.where(first, 1.0, loss_scale)
    for j in range(n_mp):
        value = blocks[j, :, :width] * jnp.exp2(blocks[j, 0:1, width : width + 1])
        value = (value * weight * scale).astype(BF16)
        for h in range(2):
            at = h * half + j * piece
            delta[at : at + piece, :] = value[h * piece : (h + 1) * piece, :]
    size = row_piece * hidden // LANES
    chunk = row_piece * 8
    turned = delta[...].T
    powers = []

    def outer(side, turned, right):
        highest = jnp.zeros((8, LANES), F32)
        for c in range(width // chunk):
            block = jnp.dot(
                turned[c * chunk : (c + 1) * chunk, :], right, preferred_element_type=F32
            )
            grads[c * chunk : (c + 1) * chunk, :] = block
            for t in range(hidden // LANES):
                lanes = jnp.abs(block[:, t * LANES : (t + 1) * LANES]).reshape(-1, 8, LANES)
                highest = jnp.maximum(highest, jnp.max(lanes, axis=0))
        power = power_of(top_of(highest))
        factor = jnp.exp2(-power)
        for owner, (slot, part) in enumerate(SLOTS):
            for t in range(hidden // LANES):
                to = (part * 2 + side) * size + t * row_piece
                out[slot, to : to + row_piece, :] = (
                    grads[
                        owner * row_piece : (owner + 1) * row_piece,
                        t * LANES : (t + 1) * LANES,
                    ]
                    * factor
                )
        powers.append(power)

    outer(1, turned, active[...])
    back = jnp.dot(delta[...], weights[...], preferred_element_type=F32)
    outer(0, normed[...].T, (back * slope[...]).astype(BF16))
    line = lax.broadcasted_iota(jnp.int32, (16, LANES), 0)
    tail = jnp.where(line < 8, powers[1], powers[0])
    for d in range(out.shape[0]):
        out[d, 4 * size :, :] = tail


def collect_kernel(place, came, own, away):
    sources = came.shape[0]
    size = (came.shape[1] - 16) // 4
    for side in range(2):
        factors = [
            jnp.exp2(came[i, 4 * size + 8 * side : 4 * size + 8 * side + 1, 0:1])
            for i in range(sources)
        ]
        for out, core in ((own, place[0]), (away, 1 - place[0])):
            at = pl.multiple_of((core * 2 + side) * size, 8)
            total = came[0, pl.ds(at, size), :] * factors[0]
            for i in range(1, sources):
                total = total + came[i, pl.ds(at, size), :] * factors[i]
            out[side * size : (side + 1) * size, :] = total


def place_kernel(place, own, came, *outs):
    rows = outs[0].shape[0]
    tiles = outs[0].shape[2] // LANES

    def run(sources):
        for out, ref in zip(outs, sources):
            for side in range(2):
                for t in range(tiles):
                    at = (side * tiles + t) * rows
                    out[:, side, t * LANES : (t + 1) * LANES] = ref[at : at + rows, :]

    pl.when(place[0] == 0)(lambda: run((own, came)))
    pl.when(place[0] != 0)(lambda: run((came, own)))


def local(
    latent_noise,
    score_noise,
    timesteps,
    classes,
    class_table,
    gen_weights,
    real_weights,
    fake_weights,
):
    group_index = lax.axis_index("group")
    core = group_index % 2
    y_lo = group_index // 2
    n_dp = lax.axis_size("dp")
    n_mp = lax.axis_size("mp")
    samples, positions, width = latent_noise.shape
    rows = positions // 2
    piece = rows // n_mp
    row_piece, _, hidden = gen_weights.shape
    loss_scale = 1.0 / math.sqrt(samples * n_dp * positions)
    place = jnp.stack([core, y_lo, lax.axis_index("mp")]).astype(jnp.int32)
    work = 2 * rows * width * hidden

    def outgoing(models):
        lanes = hidden * len(models)
        return call(
            lay_kernel, "lay", models, [], [shape((4 * n_dp, row_piece, lanes), BF16)]
        )[0]

    def gather(blocks):
        return lax.all_to_all(blocks, PLANE, 0, 0, tiled=True).reshape(width, -1)

    own_class = lax.dynamic_index_in_dim(classes, y_lo, keepdims=False)
    embedding = lax.dynamic_index_in_dim(class_table, own_class, keepdims=True).astype(F32)
    own_step = lax.dynamic_index_in_dim(timesteps, y_lo, keepdims=False)
    phase_angle = 0.5 * jnp.pi / TSTEPS * own_step.astype(F32)
    scales = jnp.stack([jnp.cos(phase_angle), jnp.sin(phase_angle)])
    prepared = call(
        lambda *refs: prepare_kernel(*refs, piece=piece),
        "prepare",
        [latent_noise, score_noise, embedding],
        [place, scales],
        [
            shape((positions, width), BF16),
            shape((2 * piece, width), F32),
            shape((2 * piece, width), F32),
        ],
    )

    gen_mine, score_blocks, prepared, embedding, scales = lax.optimization_barrier(
        (
            gather(outgoing([gen_weights])),
            outgoing([fake_weights, real_weights]),
            prepared,
            embedding,
            scales,
        )
    )
    normed_gen, stream, scaled_noise = prepared
    score_weights = gather(score_blocks)
    gen_other = core_swap(gen_mine)

    steps = n_mp // 2 - 1
    some = shape((steps * piece, width), BF16)
    one = shape((piece, width), BF16)
    two = shape((2 * piece, width), BF16)
    preact_gen, active_gen, kept, across, own, away = call(
        gen_kernel,
        "generate",
        [normed_gen, gen_mine, gen_other],
        [place],
        [shape((rows, hidden), F32), shape((rows, hidden), BF16), some, one, one, some],
        2 * work,
        [pltpu.VMEM((rows, width), BF16)],
        room=60,
    )
    joined = call(join_kernel, "join", [kept, core_swap(away)], [], [two] * steps)
    came = [paired(block, k + 1) for k, block in enumerate(joined)]
    across = paired(across, n_mp // 2)
    both_f32 = shape((2 * piece, width), F32)
    (sums,) = call(sums_kernel, "sums", [own, across] + came, [], [both_f32])
    latents, noised, noised_mine = call(
        latent_kernel,
        "latent",
        [sums, core_swap(sums), stream, scaled_noise],
        [place, scales],
        [both_f32, two, one],
    )
    blocks = [paired(noised, k + 1) for k in range(steps)]
    blocks.append(paired(noised_mine, n_mp // 2))
    (around,) = call(
        order_kernel, "order", blocks, [], [shape(((2 * steps + 1) * piece, width), BF16)]
    )
    score_weights, around = lax.optimization_barrier((score_weights, around))
    around_other = core_swap(around)
    (score_parts,) = call(
        score_kernel,
        "score",
        [noised, around, around_other, embedding, score_weights],
        [place],
        [shape((n_mp, 2 * piece, width + LANES), F32)],
        8 * work,
        [pltpu.VMEM((2 * positions, width), BF16)],
    )

    def exchange(blocks):
        return lax.all_to_all(blocks.astype(jnp.float16), "mp", 0, 0, tiled=True).astype(F32)

    (total,) = call(
        total_kernel, "total", [exchange(score_parts)], [], [shape((2 * piece, width), F32)]
    )
    (message,) = call(
        lambda *refs: pack_kernel(*refs, loss_scale=loss_scale),
        "pack",
        [total, core_swap(total), latents, noised],
        [place],
        [shape((2 * piece, width + LANES), F32)],
    )

    message, around, around_other = lax.optimization_barrier((message, around, around_other))
    normed_cond, preact_fake, active_fake = call(
        refresh_kernel,
        "refresh",
        [noised, around, around_other, embedding, score_weights],
        [place],
        [
            shape((positions, width), BF16),
            shape((positions, hidden), F32),
            shape((positions, hidden), BF16),
        ],
        2 * work,
    )
    first = core == 0

    def chosen(fake_value, gen_value):
        gen_all = jnp.concatenate([core_swap(gen_value), gen_value], axis=0)
        return jnp.where(first, fake_value, gen_all)

    preact = chosen(preact_fake, preact_gen)
    slope = jax.vjp(jax.nn.gelu, preact)[1](jnp.ones_like(preact))[0]
    size = row_piece * hidden // LANES
    (grads,) = call(
        lambda *refs: grad_kernel(
            *refs, loss_scale=loss_scale, count=positions * width, row_piece=row_piece
        ),
        "grads",
        [
            exchange(jnp.broadcast_to(message[None], (n_mp,) + message.shape)),
            jnp.where(first, score_weights[:, hidden:], gen_mine),
            slope,
            jnp.where(first, normed_cond, normed_gen),
            chosen(active_fake, active_gen),
        ],
        [place],
        [shape((len(WALK), 4 * size + 16, LANES), F32)],
        6 * work,
        [pltpu.VMEM((positions, width), BF16), pltpu.VMEM((width, hidden), F32)],
    )
    came = lax.all_to_all(
        grads.astype(jnp.float16), PLANE, 0, 0, axis_index_groups=PEERS, tiled=True
    )
    own, away = call(
        collect_kernel,
        "collect",
        [came.astype(F32)],
        [place],
        [shape((2 * size, LANES), F32)] * 2,
    )
    fake_grad, gen_grad = call(
        place_kernel,
        "place",
        [own, core_swap(away)],
        [place],
        [shape((row_piece, 2, hidden), F32)] * 2,
    )
    return (gen_grad, fake_grad)


def solution(mesh):
    return jax.shard_map(
        local,
        mesh=mesh,
        in_specs=(
            P("dp", None, None),
            P("dp", None, None),
            P("dp"),
            P("dp"),
            P(),
            P(("group", "dp"), None, "mp"),
            P(("group", "dp"), None, "mp"),
            P(("group", "dp"), None, "mp"),
        ),
        out_specs=(P(("group", "dp"), None, "mp"), P(("group", "dp"), None, "mp")),
        check_vma=False,
    )
```

```python
import math

import jax
import jax.numpy as jnp
from jax import lax
from jax.experimental import pallas as pl
from jax.experimental.pallas import tpu as pltpu
from jax.sharding import PartitionSpec as P

TSTEPS = 1000
GUIDANCE = 3.0
EPSILON = 1e-06
MEAN_EPS = 1e-05

PLANE = ("group", "dp")
LANES = 128
WALK = [(0, 0), (1, 0), (2, 0), (3, 0), (3, 1), (2, 1), (1, 1), (1, 2)]
WALK += [(2, 2), (3, 2), (3, 3), (2, 3), (1, 3), (0, 3), (0, 2), (0, 1)]
SLOTS = [
    (WALK.index((x, y_hi * 2 + y_lo)), core)
    for y_lo in range(2)
    for core in range(2)
    for x in range(4)
    for y_hi in range(2)
]
PEERS = [[((y % 2) * 2 + core) * 8 + x * 2 + y // 2 for x, y in WALK] for core in range(2)]
SMEM = pl.BlockSpec(memory_space=pltpu.SMEM)
VMEM = pl.BlockSpec(memory_space=pltpu.VMEM)
F32 = jnp.float32
BF16 = jnp.bfloat16


def call(body, name, inputs, scalars, outs, flops=0, scratch=(), room=40):
    moved = sum(math.prod(a.shape) * a.dtype.itemsize for a in list(inputs) + list(outs))
    return pl.pallas_call(
        body,
        name=name,
        out_shape=outs,
        in_specs=[SMEM] * len(scalars) + [VMEM] * len(inputs),
        out_specs=[VMEM] * len(outs),
        scratch_shapes=list(scratch),
        compiler_params=pltpu.CompilerParams(vmem_limit_bytes=room * 2**20),
        cost_estimate=pl.CostEstimate(flops=flops, bytes_accessed=moved, transcendentals=0),
    )(*scalars, *inputs)


def shape(dims, dtype):
    return jax.ShapeDtypeStruct(dims, dtype)


def normalize(summed):
    factor = lax.rsqrt(jnp.mean(summed * summed, axis=-1, keepdims=True) + EPSILON)
    return (summed * factor).astype(BF16)


def dot_t(left, right):
    return lax.dot_general(left, right, (((1,), (1,)), ((), ())), preferred_element_type=F32)


def forward_part(normed, w_in, w_out):
    preact = jnp.dot(normed, w_in, preferred_element_type=F32)
    active = jax.nn.gelu(preact).astype(BF16)
    return preact, active, dot_t(active, w_out).astype(BF16)


def core_swap(block):
    return lax.ppermute(block, "group", [(0, 1), (1, 0), (2, 3), (3, 2)])


def paired(block, step):
    n_mp = lax.axis_size("mp")
    pairs = []
    for group in range(lax.axis_size("group")):
        sign = 1 - 2 * (group % 2)
        for z in range(n_mp):
            pairs.append((group * n_mp + z, group * n_mp + (z + sign * step) % n_mp))
    return lax.ppermute(block, ("group", "mp"), pairs)


def on_core(place, run, mine, other):
    pl.when(place[0] == 0)(lambda: run(mine, other))
    pl.when(place[0] != 0)(lambda: run(other, mine))


def power_of(peak):
    return jnp.floor(jnp.log(jnp.maximum(peak, 1e-30)) * (1.0 / math.log(2.0))) - 13.0


def top_of(value):
    by_row = jnp.max(jnp.abs(value), axis=1, keepdims=True)
    return jnp.max(by_row, axis=0, keepdims=True)


def above(place, core, step, n_mp):
    return lax.rem(place[2] + n_mp + (1 - 2 * core) * step, n_mp)


def row_at(index, size):
    return pl.multiple_of(index * size, size)


def lay_kernel(*refs):
    models, out = refs[:-1], refs[-1]
    count = out.shape[0] // 4
    if len(models) == 1:
        wholes = [models[0][:, side, :] for side in range(2)]
    else:
        wholes = [jnp.concatenate([m[:, 0, :], m[:, 1, :]], axis=1) for m in models]
    for core, whole in enumerate(wholes):
        for d in range(count):
            out[core * count + d] = whole
            out[(2 + core) * count + d] = whole


def prepare_kernel(place, scales, latent, noise, embed, normed, stream, scaled, *, piece):
    rows = latent[place[1]].astype(F32)
    normed[...] = normalize(rows + embed[...])
    half = rows.shape[0] // 2
    for core in range(2):
        at = pl.multiple_of(core * half + place[2] * piece, piece)
        to = slice(core * piece, (core + 1) * piece)
        stream[to, :] = latent[place[1], pl.ds(at, piece), :].astype(F32)
        scaled[to, :] = scales[1] * noise[place[1], pl.ds(at, piece), :].astype(F32)


def gen_rows(place, core, piece, n_mp):
    half = n_mp * piece
    for k in range(1, n_mp // 2):
        for owner in range(2):
            yield pl.multiple_of(owner * half + above(place, core, k, n_mp) * piece, piece)
    for k in (0, n_mp // 2):
        yield pl.multiple_of(core * half + above(place, core, k, n_mp) * piece, piece)


def gen_kernel(place, normed, mine, other, *refs):
    preact_ref, active_ref, own, across = refs[:4]
    blocks, rows_of = refs[4:-1], refs[-1]
    piece = own.shape[0]
    n_mp = rows_of.shape[0] // piece
    for i, at in enumerate(gen_rows(place, place[0], piece, n_mp)):
        rows_of[i * piece : (i + 1) * piece, :] = normed[pl.ds(at, piece), :]

    def run(w_in, w_out):
        preact, active, partial = forward_part(rows_of[...], w_in[...], w_out[...])
        preact_ref[...] = preact
        active_ref[...] = active
        for k, block in enumerate(blocks):
            block[...] = partial[2 * k * piece : 2 * (k + 1) * piece, :]
        at = 2 * len(blocks) * piece
        own[...] = partial[at : at + piece, :]
        across[...] = partial[at + piece :, :]

    on_core(place, run, mine, other)


def sums_kernel(place, own, across, *refs):
    blocks, out = refs[:-1], refs[-1]
    piece = own.shape[0]
    total = 0.0
    for block in blocks:
        total = total + block[...].astype(F32)
    out[...] = total
    at = pl.ds(row_at(place[0], piece), piece)
    out[at, :] = out[at, :] + (own[...].astype(F32) + across[...].astype(F32))


def latent_kernel(place, scales, sums, came, stream, scaled, latents, noised, mine):
    piece = mine.shape[0]
    latents[...] = stream[...] + (sums[...] + came[...])
    noised[...] = (scales[0] * latents[...] + scaled[...]).astype(BF16)
    mine[...] = noised[pl.ds(row_at(place[0], piece), piece), :]


def rows_in_order(place, own, came, pair, store):
    piece = pair.shape[0] // 2
    n_mp = 2 * len(own)
    half = n_mp * piece

    def at(core, z):
        return pl.multiple_of(core * half + z * piece, piece)

    for core in range(2):
        store(at(core, place[2]), pair[core * piece : (core + 1) * piece, :])
    for blocks, sender in ((own, place[0]), (came, 1 - place[0])):
        for k, block in enumerate(blocks[:-1]):
            z = above(place, sender, -(k + 1), n_mp)
            for core in range(2):
                store(at(core, z), block[core * piece : (core + 1) * piece, :])
        store(at(sender, above(place, sender, n_mp // 2, n_mp)), blocks[-1][...])


def score_kernel(place, pair, *refs):
    embed, weights, out, both = refs[-4:]
    n_mp, piece = out.shape[0], out.shape[1] // 2
    own, came = refs[: n_mp // 2], refs[n_mp // 2 : n_mp]
    width = embed.shape[1]
    half = n_mp * piece
    rows = 2 * half
    hidden = weights.shape[1] // 2

    def store(at, value):
        summed = value.astype(F32)
        both[pl.ds(at, piece), :] = normalize(summed + embed[...])
        both[pl.ds(pl.multiple_of(rows + at, piece), piece), :] = normalize(summed)

    rows_in_order(place, own, came, pair, store)

    def finish(value):
        power = power_of(top_of(value))
        value = value * jnp.exp2(-power)
        tail = jnp.broadcast_to(power, (2 * piece, LANES))
        for j in range(n_mp):
            for h in range(2):
                at = h * half + j * piece
                out[j, h * piece : (h + 1) * piece, :width] = value[at : at + piece, :]
            out[j, :, width:] = tail

    @pl.when(place[0] == 0)
    def _():
        fake = forward_part(both[:rows, :], weights[:, :hidden], weights[:, hidden:])[2]
        finish(fake.astype(F32))

    @pl.when(place[0] != 0)
    def _():
        real = forward_part(both[...], weights[:, :hidden], weights[:, hidden:])[2]
        uncond, cond = real[rows:].astype(F32), real[:rows].astype(F32)
        finish(uncond + GUIDANCE * (cond - uncond))


def refresh_kernel(place, pair, *refs):
    embed, weights, normed_gen, active_own, active_came, preact_own, preact_came = refs[-10:-3]
    normed, preact, active = refs[-3:]
    piece = pair.shape[0] // 2
    n_mp = normed.shape[0] // (2 * piece)
    own, came = refs[: n_mp // 2], refs[n_mp // 2 : n_mp]
    hidden = preact.shape[1]

    def store(at, value):
        normed[pl.ds(at, piece), :] = normalize(value.astype(F32) + embed[...])

    @pl.when(place[0] == 0)
    def _():
        rows_in_order(place, own, came, pair, store)
        preact[...] = jnp.dot(normed[...], weights[:, :hidden], preferred_element_type=F32)
        active[...] = jax.nn.gelu(preact[...]).astype(BF16)

    @pl.when(place[0] != 0)
    def _():
        normed[...] = normed_gen[...]
        for core, acts, pres in ((1, active_own, preact_own), (0, active_came, preact_came)):
            for i, at in enumerate(gen_rows(place, core, piece, n_mp)):
                active[pl.ds(at, piece), :] = acts[i * piece : (i + 1) * piece, :]
                preact[pl.ds(at, piece), :] = pres[i * piece : (i + 1) * piece, :]


def total_kernel(blocks, out):
    width = out.shape[1]
    total = 0.0
    for j in range(blocks.shape[0]):
        total = total + blocks[j, :, :width] * jnp.exp2(blocks[j, 0:1, width : width + 1])
    out[...] = total


def pack_kernel(place, own, other, latents_ref, noised, out, *, loss_scale):
    width = own.shape[1]
    piece = own.shape[0] // 2
    first = place[0] == 0

    def run(fake_sum, real_sum):
        latents = latents_ref[...]
        base = noised[...].astype(F32)
        fake = base + fake_sum[...]
        real_mix = base + real_sum[...]
        away = jnp.sum(jnp.abs(latents - real_mix), axis=1, keepdims=True)
        gap = jnp.sum(away, axis=0, keepdims=True)
        fake_delta = (2.0 * (fake - latents) * loss_scale).astype(BF16).astype(F32)
        value = jnp.where(first, fake_delta, fake - real_mix)
        power = power_of(top_of(value))
        out[:, :width] = value * jnp.exp2(-power)
        gap_power = power_of(gap)
        scaled = gap * jnp.exp2(-gap_power)
        coarse = jnp.floor(scaled * (1.0 / 16.0)) * 16.0
        line = lax.broadcasted_iota(jnp.int32, (2 * piece, LANES), 0)
        tail = jnp.where(line == 8, gap_power, power)
        tail = jnp.where(line == 9, coarse, tail)
        out[:, width:] = jnp.where(line == 10, scaled - coarse, tail)

    pl.when(first)(lambda: run(own, other))
    pl.when(place[0] != 0)(lambda: run(other, own))


def grad_kernel(
    place, blocks, weights, slope, normed, active, out, delta, grads, *, loss_scale, count, row_piece
):
    n_mp, piece = blocks.shape[0], blocks.shape[1] // 2
    rows, width = normed.shape
    hidden = active.shape[1]
    half = rows // 2
    gap = 0.0
    for j in range(n_mp):
        tail = blocks[j, :, width:]
        gap = gap + (tail[9:10, 0:1] + tail[10:11, 0:1]) * jnp.exp2(tail[8:9, 0:1])
    first = place[0] == 0
    weight = jnp.where(first, 1.0, 1.0 / (gap / count + MEAN_EPS))
    scale = jnp.where(first, 1.0, loss_scale)
    for j in range(n_mp):
        value = blocks[j, :, :width] * jnp.exp2(blocks[j, 0:1, width : width + 1])
        value = (value * weight * scale).astype(BF16)
        for h in range(2):
            at = h * half + j * piece
            delta[at : at + piece, :] = value[h * piece : (h + 1) * piece, :]
    size = row_piece * hidden // LANES
    chunk = row_piece * 8
    turned = delta[...].T
    powers = []

    def outer(side, turned, right):
        highest = jnp.zeros((8, LANES), F32)
        for c in range(width // chunk):
            block = jnp.dot(
                turned[c * chunk : (c + 1) * chunk, :], right, preferred_element_type=F32
            )
            grads[c * chunk : (c + 1) * chunk, :] = block
            for t in range(hidden // LANES):
                lanes = jnp.abs(block[:, t * LANES : (t + 1) * LANES]).reshape(-1, 8, LANES)
                highest = jnp.maximum(highest, jnp.max(lanes, axis=0))
        power = power_of(top_of(highest))
        factor = jnp.exp2(-power)
        for owner, (slot, part) in enumerate(SLOTS):
            for t in range(hidden // LANES):
                to = (part * 2 + side) * size + t * row_piece
                out[slot, to : to + row_piece, :] = (
                    grads[
                        owner * row_piece : (owner + 1) * row_piece,
                        t * LANES : (t + 1) * LANES,
                    ]
                    * factor
                )
        powers.append(power)

    outer(1, turned, active[...])
    back = jnp.dot(delta[...], weights[...], preferred_element_type=F32)
    outer(0, normed[...].T, (back * slope[...]).astype(BF16))
    line = lax.broadcasted_iota(jnp.int32, (16, LANES), 0)
    tail = jnp.where(line < 8, powers[1], powers[0])
    for d in range(out.shape[0]):
        out[d, 4 * size :, :] = tail


def collect_kernel(place, came, own, away):
    sources = came.shape[0]
    size = (came.shape[1] - 16) // 4
    for side in range(2):
        factors = [
            jnp.exp2(came[i, 4 * size + 8 * side : 4 * size + 8 * side + 1, 0:1])
            for i in range(sources)
        ]
        for out, core in ((own, place[0]), (away, 1 - place[0])):
            at = pl.multiple_of((core * 2 + side) * size, 8)
            total = came[0, pl.ds(at, size), :] * factors[0]
            for i in range(1, sources):
                total = total + came[i, pl.ds(at, size), :] * factors[i]
            out[side * size : (side + 1) * size, :] = total


def place_kernel(place, own, came, *outs):
    rows = outs[0].shape[0]
    tiles = outs[0].shape[2] // LANES

    def run(sources):
        for out, ref in zip(outs, sources):
            for side in range(2):
                for t in range(tiles):
                    at = (side * tiles + t) * rows
                    out[:, side, t * LANES : (t + 1) * LANES] = ref[at : at + rows, :]

    pl.when(place[0] == 0)(lambda: run((own, came)))
    pl.when(place[0] != 0)(lambda: run((came, own)))


def local(
    latent_noise,
    score_noise,
    timesteps,
    classes,
    class_table,
    gen_weights,
    real_weights,
    fake_weights,
):
    group_index = lax.axis_index("group")
    core = group_index % 2
    y_lo = group_index // 2
    n_dp = lax.axis_size("dp")
    n_mp = lax.axis_size("mp")
    samples, positions, width = latent_noise.shape
    rows = positions // 2
    piece = rows // n_mp
    row_piece, _, hidden = gen_weights.shape
    loss_scale = 1.0 / math.sqrt(samples * n_dp * positions)
    place = jnp.stack([core, y_lo, lax.axis_index("mp")]).astype(jnp.int32)
    work = 2 * rows * width * hidden

    def outgoing(models):
        lanes = hidden * len(models)
        blocks = [shape((4 * n_dp, row_piece, lanes), BF16)]
        return call(lay_kernel, "lay", models, [], blocks, room=60)[0]

    def gather(blocks):
        return lax.all_to_all(blocks, PLANE, 0, 0, tiled=True).reshape(width, -1)

    own_class = lax.dynamic_index_in_dim(classes, y_lo, keepdims=False)
    embedding = lax.dynamic_index_in_dim(class_table, own_class, keepdims=True).astype(F32)
    own_step = lax.dynamic_index_in_dim(timesteps, y_lo, keepdims=False)
    phase_angle = 0.5 * jnp.pi / TSTEPS * own_step.astype(F32)
    scales = jnp.stack([jnp.cos(phase_angle), jnp.sin(phase_angle)])
    prepared = call(
        lambda *refs: prepare_kernel(*refs, piece=piece),
        "prepare",
        [latent_noise, score_noise, embedding],
        [place, scales],
        [
            shape((positions, width), BF16),
            shape((2 * piece, width), F32),
            shape((2 * piece, width), F32),
        ],
    )

    gen_mine, score_blocks, prepared, embedding, scales = lax.optimization_barrier(
        (
            gather(outgoing([gen_weights])),
            outgoing([fake_weights, real_weights]),
            prepared,
            embedding,
            scales,
        )
    )
    normed_gen, stream, scaled_noise = prepared
    score_weights = gather(score_blocks)
    gen_other = core_swap(gen_mine)

    steps = n_mp // 2 - 1
    one = shape((piece, width), BF16)
    two = shape((2 * piece, width), BF16)
    preact_gen, active_gen, own, across, *sent = call(
        gen_kernel,
        "generate",
        [normed_gen, gen_mine, gen_other],
        [place],
        [shape((rows, hidden), F32), shape((rows, hidden), BF16), one, one] + [two] * steps,
        2 * work,
        [pltpu.VMEM((rows, width), BF16)],
        room=60,
    )
    came = [paired(block, k + 1) for k, block in enumerate(sent)]
    across = paired(across, n_mp // 2)
    both_f32 = shape((2 * piece, width), F32)
    (sums,) = call(sums_kernel, "sums", [own, across] + came, [place], [both_f32], room=60)
    latents, noised, noised_mine = call(
        latent_kernel,
        "latent",
        [sums, core_swap(sums), stream, scaled_noise],
        [place, scales],
        [both_f32, two, one],
        room=60,
    )
    around = [paired(noised, k + 1) for k in range(steps)]
    around.append(paired(noised_mine, n_mp // 2))
    around += [core_swap(block) for block in around]
    score_weights, around = lax.optimization_barrier((score_weights, around))
    (score_parts,) = call(
        score_kernel,
        "score",
        [noised] + around + [embedding, score_weights],
        [place],
        [shape((n_mp, 2 * piece, width + LANES), F32)],
        8 * work,
        [pltpu.VMEM((2 * positions, width), BF16)],
    )

    def exchange(blocks):
        return lax.all_to_all(blocks.astype(jnp.float16), "mp", 0, 0, tiled=True).astype(F32)

    (total,) = call(
        total_kernel, "total", [exchange(score_parts)], [], [shape((2 * piece, width), F32)]
    )
    (message,) = call(
        lambda *refs: pack_kernel(*refs, loss_scale=loss_scale),
        "pack",
        [total, core_swap(total), latents, noised],
        [place],
        [shape((2 * piece, width + LANES), F32)],
        room=60,
    )

    message, around = lax.optimization_barrier((message, around))
    normed, preact, active = call(
        refresh_kernel,
        "refresh",
        [noised]
        + around
        + [embedding, score_weights, normed_gen]
        + [active_gen, core_swap(active_gen), preact_gen, core_swap(preact_gen)],
        [place],
        [
            shape((positions, width), BF16),
            shape((positions, hidden), F32),
            shape((positions, hidden), BF16),
        ],
        2 * work,
    )
    slope = jax.vjp(jax.nn.gelu, preact)[1](jnp.ones_like(preact))[0]
    size = row_piece * hidden // LANES
    (grads,) = call(
        lambda *refs: grad_kernel(
            *refs, loss_scale=loss_scale, count=positions * width, row_piece=row_piece
        ),
        "grads",
        [
            exchange(jnp.broadcast_to(message[None], (n_mp,) + message.shape)),
            jnp.where(core == 0, score_weights[:, hidden:], gen_mine),
            slope,
            normed,
            active,
        ],
        [place],
        [shape((len(WALK), 4 * size + 16, LANES), F32)],
        6 * work,
        [pltpu.VMEM((positions, width), BF16), pltpu.VMEM((width, hidden), F32)],
    )
    came = lax.all_to_all(
        grads.astype(jnp.float16), PLANE, 0, 0, axis_index_groups=PEERS, tiled=True
    )
    own, away = call(
        collect_kernel,
        "collect",
        [came.astype(F32)],
        [place],
        [shape((2 * size, LANES), F32)] * 2,
    )
    fake_grad, gen_grad = call(
        place_kernel,
        "place",
        [own, core_swap(away)],
        [place],
        [shape((row_piece, 2, hidden), F32)] * 2,
    )
    return (gen_grad, fake_grad)


def solution(mesh):
    return jax.shard_map(
        local,
        mesh=mesh,
        in_specs=(
            P("dp", None, None),
            P("dp", None, None),
            P("dp"),
            P("dp"),
            P(),
            P(("group", "dp"), None, "mp"),
            P(("group", "dp"), None, "mp"),
            P(("group", "dp"), None, "mp"),
        ),
        out_specs=(P(("group", "dp"), None, "mp"), P(("group", "dp"), None, "mp")),
        check_vma=False,
    )
```

```python
import math

import jax
import jax.numpy as jnp
from jax import lax
from jax.experimental import pallas as pl
from jax.experimental.pallas import tpu as pltpu
from jax.sharding import PartitionSpec as P

TSTEPS = 1000
GUIDANCE = 3.0
EPSILON = 1e-06
MEAN_EPS = 1e-05

PLANE = ("group", "dp")
LANES = 128
WALK = [(0, 0), (1, 0), (2, 0), (3, 0), (3, 1), (2, 1), (1, 1), (1, 2)]
WALK += [(2, 2), (3, 2), (3, 3), (2, 3), (1, 3), (0, 3), (0, 2), (0, 1)]
SLOTS = [
    (WALK.index((x, y_hi * 2 + y_lo)), core)
    for y_lo in range(2)
    for core in range(2)
    for x in range(4)
    for y_hi in range(2)
]
PEERS = [[((y % 2) * 2 + core) * 8 + x * 2 + y // 2 for x, y in WALK] for core in range(2)]
SMEM = pl.BlockSpec(memory_space=pltpu.SMEM)
VMEM = pl.BlockSpec(memory_space=pltpu.VMEM)
F32 = jnp.float32
BF16 = jnp.bfloat16


def call(body, name, inputs, scalars, outs, flops=0, scratch=(), room=40):
    moved = sum(math.prod(a.shape) * a.dtype.itemsize for a in list(inputs) + list(outs))
    return pl.pallas_call(
        body,
        name=name,
        out_shape=outs,
        in_specs=[SMEM] * len(scalars) + [VMEM] * len(inputs),
        out_specs=[VMEM] * len(outs),
        scratch_shapes=list(scratch),
        compiler_params=pltpu.CompilerParams(vmem_limit_bytes=room * 2**20),
        cost_estimate=pl.CostEstimate(flops=flops, bytes_accessed=moved, transcendentals=0),
    )(*scalars, *inputs)


def shape(dims, dtype):
    return jax.ShapeDtypeStruct(dims, dtype)


def normalize(summed):
    factor = lax.rsqrt(jnp.mean(summed * summed, axis=-1, keepdims=True) + EPSILON)
    return (summed * factor).astype(BF16)


def dot_t(left, right):
    return lax.dot_general(left, right, (((1,), (1,)), ((), ())), preferred_element_type=F32)


def forward_part(normed, w_in, w_out):
    preact = jnp.dot(normed, w_in, preferred_element_type=F32)
    active = jax.nn.gelu(preact).astype(BF16)
    return preact, active, dot_t(active, w_out).astype(BF16)


def core_swap(block):
    return lax.ppermute(block, "group", [(0, 1), (1, 0), (2, 3), (3, 2)])


def paired(block, step):
    n_mp = lax.axis_size("mp")
    pairs = []
    for group in range(lax.axis_size("group")):
        sign = 1 - 2 * (group % 2)
        for z in range(n_mp):
            pairs.append((group * n_mp + z, group * n_mp + (z + sign * step) % n_mp))
    return lax.ppermute(block, ("group", "mp"), pairs)


def on_core(place, run, mine, other):
    pl.when(place[0] == 0)(lambda: run(mine, other))
    pl.when(place[0] != 0)(lambda: run(other, mine))


def power_of(peak):
    return jnp.floor(jnp.log(jnp.maximum(peak, 1e-30)) * (1.0 / math.log(2.0))) - 13.0


def top_of(value):
    by_row = jnp.max(jnp.abs(value), axis=1, keepdims=True)
    return jnp.max(by_row, axis=0, keepdims=True)


def above(place, core, step, n_mp):
    return lax.rem(place[2] + n_mp + (1 - 2 * core) * step, n_mp)


def row_at(index, size):
    return pl.multiple_of(index * size, size)


def lay_kernel(*refs):
    models, out = refs[:-1], refs[-1]
    count = out.shape[0] // 4
    if len(models) == 1:
        wholes = [models[0][:, side, :] for side in range(2)]
    else:
        wholes = [jnp.concatenate([m[:, 0, :], m[:, 1, :]], axis=1) for m in models]
    for core, whole in enumerate(wholes):
        for d in range(count):
            out[core * count + d] = whole
            out[(2 + core) * count + d] = whole


def prepare_kernel(place, scales, latent, noise, embed, normed, stream, scaled, *, piece):
    rows = latent[place[1]].astype(F32)
    normed[...] = normalize(rows + embed[...])
    half = rows.shape[0] // 2
    for core in range(2):
        at = pl.multiple_of(core * half + place[2] * piece, piece)
        to = slice(core * piece, (core + 1) * piece)
        stream[to, :] = latent[place[1], pl.ds(at, piece), :].astype(F32)
        scaled[to, :] = scales[1] * noise[place[1], pl.ds(at, piece), :].astype(F32)


def gen_rows(place, core, piece, n_mp):
    half = n_mp * piece
    for k in range(1, n_mp // 2):
        for owner in range(2):
            yield pl.multiple_of(owner * half + above(place, core, k, n_mp) * piece, piece)
    for k in (0, n_mp // 2):
        yield pl.multiple_of(core * half + above(place, core, k, n_mp) * piece, piece)


def gen_kernel(place, normed, mine, other, *refs):
    preact_ref, active_ref, own, across = refs[:4]
    blocks, rows_of = refs[4:-1], refs[-1]
    piece = own.shape[0]
    n_mp = rows_of.shape[0] // piece
    for i, at in enumerate(gen_rows(place, place[0], piece, n_mp)):
        rows_of[i * piece : (i + 1) * piece, :] = normed[pl.ds(at, piece), :]

    def run(w_in, w_out):
        preact, active, partial = forward_part(rows_of[...], w_in[...], w_out[...])
        preact_ref[...] = preact
        active_ref[...] = active
        for k, block in enumerate(blocks):
            block[...] = partial[2 * k * piece : 2 * (k + 1) * piece, :]
        at = 2 * len(blocks) * piece
        own[...] = partial[at : at + piece, :]
        across[...] = partial[at + piece :, :]

    on_core(place, run, mine, other)


def sums_kernel(place, own, across, *refs):
    blocks, out = refs[:-1], refs[-1]
    piece = own.shape[0]
    total = 0.0
    for block in blocks:
        total = total + block[...].astype(F32)
    out[...] = total
    at = pl.ds(row_at(place[0], piece), piece)
    out[at, :] = out[at, :] + (own[...].astype(F32) + across[...].astype(F32))


def latent_kernel(place, scales, sums, came, stream, scaled, latents, noised, mine):
    piece = mine.shape[0]
    latents[...] = stream[...] + (sums[...] + came[...])
    noised[...] = (scales[0] * latents[...] + scaled[...]).astype(BF16)
    mine[...] = noised[pl.ds(row_at(place[0], piece), piece), :]


def order_kernel(*refs):
    blocks, out = refs[:-1], refs[-1]
    at = 0
    for block in blocks:
        out[at : at + block.shape[0], :] = block[...]
        at += block.shape[0]


def rows_in_order(place, own, came, pair, store):
    piece = pair.shape[0] // 2
    n_mp = (own.shape[0] // piece + 1) // 2 * 2
    half = n_mp * piece

    def at(core, z):
        return pl.multiple_of(core * half + z * piece, piece)

    for core in range(2):
        store(at(core, place[2]), pair[core * piece : (core + 1) * piece, :])
    for source, sender in ((own, place[0]), (came, 1 - place[0])):
        for k in range(1, n_mp // 2):
            z = above(place, sender, -k, n_mp)
            for core in range(2):
                to = ((k - 1) * 2 + core) * piece
                store(at(core, z), source[to : to + piece, :])
        to = (n_mp - 2) * piece
        store(at(sender, above(place, sender, n_mp // 2, n_mp)), source[to : to + piece, :])


def score_kernel(place, pair, own, came, embed, weights, out, both):
    n_mp, piece = out.shape[0], out.shape[1] // 2
    width = embed.shape[1]
    half = n_mp * piece
    rows = 2 * half
    hidden = weights.shape[1] // 2

    def store(at, value):
        summed = value.astype(F32)
        both[pl.ds(at, piece), :] = normalize(summed + embed[...])
        both[pl.ds(pl.multiple_of(rows + at, piece), piece), :] = normalize(summed)

    rows_in_order(place, own, came, pair, store)

    def finish(value):
        power = power_of(top_of(value))
        value = value * jnp.exp2(-power)
        tail = jnp.broadcast_to(power, (2 * piece, LANES))
        for j in range(n_mp):
            for h in range(2):
                at = h * half + j * piece
                out[j, h * piece : (h + 1) * piece, :width] = value[at : at + piece, :]
            out[j, :, width:] = tail

    @pl.when(place[0] == 0)
    def _():
        fake = forward_part(both[:rows, :], weights[:, :hidden], weights[:, hidden:])[2]
        finish(fake.astype(F32))

    @pl.when(place[0] != 0)
    def _():
        real = forward_part(both[...], weights[:, :hidden], weights[:, hidden:])[2]
        uncond, cond = real[rows:].astype(F32), real[:rows].astype(F32)
        finish(uncond + GUIDANCE * (cond - uncond))


def refresh_kernel(place, pair, own, came, *refs):
    embed, weights, normed_gen, active_own, active_came, preact_own, preact_came = refs[-10:-3]
    normed, preact, active = refs[-3:]
    piece = pair.shape[0] // 2
    n_mp = normed.shape[0] // (2 * piece)
    hidden = preact.shape[1]

    def store(at, value):
        normed[pl.ds(at, piece), :] = normalize(value.astype(F32) + embed[...])

    @pl.when(place[0] == 0)
    def _():
        rows_in_order(place, own, came, pair, store)
        preact[...] = jnp.dot(normed[...], weights[:, :hidden], preferred_element_type=F32)
        active[...] = jax.nn.gelu(preact[...]).astype(BF16)

    @pl.when(place[0] != 0)
    def _():
        normed[...] = normed_gen[...]
        for core, acts, pres in ((1, active_own, preact_own), (0, active_came, preact_came)):
            for i, at in enumerate(gen_rows(place, core, piece, n_mp)):
                active[pl.ds(at, piece), :] = acts[i * piece : (i + 1) * piece, :]
                preact[pl.ds(at, piece), :] = pres[i * piece : (i + 1) * piece, :]


def total_kernel(blocks, out):
    width = out.shape[1]
    total = 0.0
    for j in range(blocks.shape[0]):
        total = total + blocks[j, :, :width] * jnp.exp2(blocks[j, 0:1, width : width + 1])
    out[...] = total


def pack_kernel(place, own, other, latents_ref, noised, out, *, loss_scale):
    width = own.shape[1]
    piece = own.shape[0] // 2
    first = place[0] == 0

    def run(fake_sum, real_sum):
        latents = latents_ref[...]
        base = noised[...].astype(F32)
        fake = base + fake_sum[...]
        real_mix = base + real_sum[...]
        away = jnp.sum(jnp.abs(latents - real_mix), axis=1, keepdims=True)
        gap = jnp.sum(away, axis=0, keepdims=True)
        fake_delta = (2.0 * (fake - latents) * loss_scale).astype(BF16).astype(F32)
        value = jnp.where(first, fake_delta, fake - real_mix)
        power = power_of(top_of(value))
        out[:, :width] = value * jnp.exp2(-power)
        gap_power = power_of(gap)
        scaled = gap * jnp.exp2(-gap_power)
        coarse = jnp.floor(scaled * (1.0 / 16.0)) * 16.0
        line = lax.broadcasted_iota(jnp.int32, (2 * piece, LANES), 0)
        tail = jnp.where(line == 8, gap_power, power)
        tail = jnp.where(line == 9, coarse, tail)
        out[:, width:] = jnp.where(line == 10, scaled - coarse, tail)

    pl.when(first)(lambda: run(own, other))
    pl.when(place[0] != 0)(lambda: run(other, own))


def grad_kernel(
    place, blocks, weights, slope, normed, active, out, delta, grads, *, loss_scale, count, row_piece
):
    n_mp, piece = blocks.shape[0], blocks.shape[1] // 2
    rows, width = normed.shape
    hidden = active.shape[1]
    half = rows // 2
    gap = 0.0
    for j in range(n_mp):
        tail = blocks[j, :, width:]
        gap = gap + (tail[9:10, 0:1] + tail[10:11, 0:1]) * jnp.exp2(tail[8:9, 0:1])
    first = place[0] == 0
    weight = jnp.where(first, 1.0, 1.0 / (gap / count + MEAN_EPS))
    scale = jnp.where(first, 1.0, loss_scale)
    for j in range(n_mp):
        value = blocks[j, :, :width] * jnp.exp2(blocks[j, 0:1, width : width + 1])
        value = (value * weight * scale).astype(BF16)
        for h in range(2):
            at = h * half + j * piece
            delta[at : at + piece, :] = value[h * piece : (h + 1) * piece, :]
    size = row_piece * hidden // LANES
    chunk = row_piece * 8
    turned = delta[...].T
    powers = []

    def outer(side, turned, right):
        highest = jnp.zeros((8, LANES), F32)
        for c in range(width // chunk):
            block = jnp.dot(
                turned[c * chunk : (c + 1) * chunk, :], right, preferred_element_type=F32
            )
            grads[c * chunk : (c + 1) * chunk, :] = block
            for t in range(hidden // LANES):
                lanes = jnp.abs(block[:, t * LANES : (t + 1) * LANES]).reshape(-1, 8, LANES)
                highest = jnp.maximum(highest, jnp.max(lanes, axis=0))
        power = power_of(top_of(highest))
        factor = jnp.exp2(-power)
        for owner, (slot, part) in enumerate(SLOTS):
            for t in range(hidden // LANES):
                to = (part * 2 + side) * size + t * row_piece
                out[slot, to : to + row_piece, :] = (
                    grads[
                        owner * row_piece : (owner + 1) * row_piece,
                        t * LANES : (t + 1) * LANES,
                    ]
                    * factor
                )
        powers.append(power)

    outer(1, turned, active[...])
    back = jnp.dot(delta[...], weights[...], preferred_element_type=F32)
    outer(0, normed[...].T, (back * slope[...]).astype(BF16))
    line = lax.broadcasted_iota(jnp.int32, (16, LANES), 0)
    tail = jnp.where(line < 8, powers[1], powers[0])
    for d in range(out.shape[0]):
        out[d, 4 * size :, :] = tail


def collect_kernel(place, came, own, away):
    sources = came.shape[0]
    size = (came.shape[1] - 16) // 4
    for side in range(2):
        factors = [
            jnp.exp2(came[i, 4 * size + 8 * side : 4 * size + 8 * side + 1, 0:1])
            for i in range(sources)
        ]
        for out, core in ((own, place[0]), (away, 1 - place[0])):
            at = pl.multiple_of((core * 2 + side) * size, 8)
            total = came[0, pl.ds(at, size), :] * factors[0]
            for i in range(1, sources):
                total = total + came[i, pl.ds(at, size), :] * factors[i]
            out[side * size : (side + 1) * size, :] = total


def place_kernel(place, own, came, *outs):
    rows = outs[0].shape[0]
    tiles = outs[0].shape[2] // LANES

    def run(sources):
        for out, ref in zip(outs, sources):
            for side in range(2):
                for t in range(tiles):
                    at = (side * tiles + t) * rows
                    out[:, side, t * LANES : (t + 1) * LANES] = ref[at : at + rows, :]

    pl.when(place[0] == 0)(lambda: run((own, came)))
    pl.when(place[0] != 0)(lambda: run((came, own)))


def local(
    latent_noise,
    score_noise,
    timesteps,
    classes,
    class_table,
    gen_weights,
    real_weights,
    fake_weights,
):
    group_index = lax.axis_index("group")
    core = group_index % 2
    y_lo = group_index // 2
    n_dp = lax.axis_size("dp")
    n_mp = lax.axis_size("mp")
    samples, positions, width = latent_noise.shape
    rows = positions // 2
    piece = rows // n_mp
    row_piece, _, hidden = gen_weights.shape
    loss_scale = 1.0 / math.sqrt(samples * n_dp * positions)
    place = jnp.stack([core, y_lo, lax.axis_index("mp")]).astype(jnp.int32)
    work = 2 * rows * width * hidden

    def outgoing(models):
        lanes = hidden * len(models)
        blocks = [shape((4 * n_dp, row_piece, lanes), BF16)]
        return call(lay_kernel, "lay", models, [], blocks)[0]

    def gather(blocks):
        return lax.all_to_all(blocks, PLANE, 0, 0, tiled=True).reshape(width, -1)

    own_class = lax.dynamic_index_in_dim(classes, y_lo, keepdims=False)
    embedding = lax.dynamic_index_in_dim(class_table, own_class, keepdims=True).astype(F32)
    own_step = lax.dynamic_index_in_dim(timesteps, y_lo, keepdims=False)
    phase_angle = 0.5 * jnp.pi / TSTEPS * own_step.astype(F32)
    scales = jnp.stack([jnp.cos(phase_angle), jnp.sin(phase_angle)])
    prepared = call(
        lambda *refs: prepare_kernel(*refs, piece=piece),
        "prepare",
        [latent_noise, score_noise, embedding],
        [place, scales],
        [
            shape((positions, width), BF16),
            shape((2 * piece, width), F32),
            shape((2 * piece, width), F32),
        ],
    )

    gen_mine, score_blocks, prepared, embedding, scales = lax.optimization_barrier(
        (
            gather(outgoing([gen_weights])),
            outgoing([fake_weights, real_weights]),
            prepared,
            embedding,
            scales,
        )
    )
    normed_gen, stream, scaled_noise = prepared
    score_weights = gather(score_blocks)
    gen_other = core_swap(gen_mine)

    steps = n_mp // 2 - 1
    one = shape((piece, width), BF16)
    two = shape((2 * piece, width), BF16)
    preact_gen, active_gen, own, across, *sent = call(
        gen_kernel,
        "generate",
        [normed_gen, gen_mine, gen_other],
        [place],
        [shape((rows, hidden), F32), shape((rows, hidden), BF16), one, one] + [two] * steps,
        2 * work,
        [pltpu.VMEM((rows, width), BF16)],
        room=60,
    )
    came = [paired(block, k + 1) for k, block in enumerate(sent)]
    across = paired(across, n_mp // 2)
    both_f32 = shape((2 * piece, width), F32)
    (sums,) = call(sums_kernel, "sums", [own, across] + came, [place], [both_f32])
    latents, noised, noised_mine = call(
        latent_kernel,
        "latent",
        [sums, core_swap(sums), stream, scaled_noise],
        [place, scales],
        [both_f32, two, one],
    )
    around = [paired(noised, k + 1) for k in range(steps)]
    around.append(paired(noised_mine, n_mp // 2))
    (around,) = call(
        order_kernel, "order", around, [], [shape(((2 * steps + 1) * piece, width), BF16)]
    )
    score_weights, around = lax.optimization_barrier((score_weights, around))
    around_other = core_swap(around)
    (score_parts,) = call(
        score_kernel,
        "score",
        [noised, around, around_other, embedding, score_weights],
        [place],
        [shape((n_mp, 2 * piece, width + LANES), F32)],
        8 * work,
        [pltpu.VMEM((2 * positions, width), BF16)],
    )

    def exchange(blocks):
        return lax.all_to_all(blocks.astype(jnp.float16), "mp", 0, 0, tiled=True).astype(F32)

    (total,) = call(
        total_kernel, "total", [exchange(score_parts)], [], [shape((2 * piece, width), F32)]
    )
    (message,) = call(
        lambda *refs: pack_kernel(*refs, loss_scale=loss_scale),
        "pack",
        [total, core_swap(total), latents, noised],
        [place],
        [shape((2 * piece, width + LANES), F32)],
    )

    message, around, around_other = lax.optimization_barrier((message, around, around_other))
    normed, preact, active = call(
        refresh_kernel,
        "refresh",
        [noised, around, around_other, embedding, score_weights, normed_gen]
        + [active_gen, core_swap(active_gen), preact_gen, core_swap(preact_gen)],
        [place],
        [
            shape((positions, width), BF16),
            shape((positions, hidden), F32),
            shape((positions, hidden), BF16),
        ],
        2 * work,
    )
    slope = jax.vjp(jax.nn.gelu, preact)[1](jnp.ones_like(preact))[0]
    size = row_piece * hidden // LANES
    (grads,) = call(
        lambda *refs: grad_kernel(
            *refs, loss_scale=loss_scale, count=positions * width, row_piece=row_piece
        ),
        "grads",
        [
            exchange(jnp.broadcast_to(message[None], (n_mp,) + message.shape)),
            jnp.where(core == 0, score_weights[:, hidden:], gen_mine),
            slope,
            normed,
            active,
        ],
        [place],
        [shape((len(WALK), 4 * size + 16, LANES), F32)],
        6 * work,
        [pltpu.VMEM((positions, width), BF16), pltpu.VMEM((width, hidden), F32)],
    )
    came = lax.all_to_all(
        grads.astype(jnp.float16), PLANE, 0, 0, axis_index_groups=PEERS, tiled=True
    )
    own, away = call(
        collect_kernel,
        "collect",
        [came.astype(F32)],
        [place],
        [shape((2 * size, LANES), F32)] * 2,
    )
    fake_grad, gen_grad = call(
        place_kernel,
        "place",
        [own, core_swap(away)],
        [place],
        [shape((row_piece, 2, hidden), F32)] * 2,
    )
    return (gen_grad, fake_grad)


def solution(mesh):
    return jax.shard_map(
        local,
        mesh=mesh,
        in_specs=(
            P("dp", None, None),
            P("dp", None, None),
            P("dp"),
            P("dp"),
            P(),
            P(("group", "dp"), None, "mp"),
            P(("group", "dp"), None, "mp"),
            P(("group", "dp"), None, "mp"),
        ),
        out_specs=(P(("group", "dp"), None, "mp"), P(("group", "dp"), None, "mp")),
        check_vma=False,
    )
```

```python
import math

import jax
import jax.numpy as jnp
from jax import lax
from jax.experimental import pallas as pl
from jax.experimental.pallas import tpu as pltpu
from jax.sharding import PartitionSpec as P

TSTEPS = 1000
GUIDANCE = 3.0
EPSILON = 1e-06
MEAN_EPS = 1e-05

PLANE = ("group", "dp")
LANES = 128
WALK = [(0, 0), (1, 0), (2, 0), (3, 0), (3, 1), (2, 1), (1, 1), (1, 2)]
WALK += [(2, 2), (3, 2), (3, 3), (2, 3), (1, 3), (0, 3), (0, 2), (0, 1)]
SLOTS = [
    (WALK.index((x, y_hi * 2 + y_lo)), core)
    for y_lo in range(2)
    for core in range(2)
    for x in range(4)
    for y_hi in range(2)
]
PEERS = [[((y % 2) * 2 + core) * 8 + x * 2 + y // 2 for x, y in WALK] for core in range(2)]
SMEM = pl.BlockSpec(memory_space=pltpu.SMEM)
VMEM = pl.BlockSpec(memory_space=pltpu.VMEM)
F32 = jnp.float32
BF16 = jnp.bfloat16


def call(body, name, inputs, scalars, outs, flops=0, scratch=(), room=40):
    moved = sum(math.prod(a.shape) * a.dtype.itemsize for a in list(inputs) + list(outs))
    return pl.pallas_call(
        body,
        name=name,
        out_shape=outs,
        in_specs=[SMEM] * len(scalars) + [VMEM] * len(inputs),
        out_specs=[VMEM] * len(outs),
        scratch_shapes=list(scratch),
        compiler_params=pltpu.CompilerParams(vmem_limit_bytes=room * 2**20),
        cost_estimate=pl.CostEstimate(flops=flops, bytes_accessed=moved, transcendentals=0),
    )(*scalars, *inputs)


def shape(dims, dtype):
    return jax.ShapeDtypeStruct(dims, dtype)


def normalize(summed):
    factor = lax.rsqrt(jnp.mean(summed * summed, axis=-1, keepdims=True) + EPSILON)
    return (summed * factor).astype(BF16)


def dot_t(left, right):
    return lax.dot_general(left, right, (((1,), (1,)), ((), ())), preferred_element_type=F32)


def forward_part(normed, w_in, w_out):
    preact = jnp.dot(normed, w_in, preferred_element_type=F32)
    active = jax.nn.gelu(preact).astype(BF16)
    return preact, active, dot_t(active, w_out).astype(BF16)


def core_swap(block):
    return lax.ppermute(block, "group", [(0, 1), (1, 0), (2, 3), (3, 2)])


def paired(block, step):
    n_mp = lax.axis_size("mp")
    pairs = []
    for group in range(lax.axis_size("group")):
        sign = 1 - 2 * (group % 2)
        for z in range(n_mp):
            pairs.append((group * n_mp + z, group * n_mp + (z + sign * step) % n_mp))
    return lax.ppermute(block, ("group", "mp"), pairs)


def on_core(place, run, mine, other):
    pl.when(place[0] == 0)(lambda: run(mine, other))
    pl.when(place[0] != 0)(lambda: run(other, mine))


def power_of(peak):
    return jnp.floor(jnp.log(jnp.maximum(peak, 1e-30)) * (1.0 / math.log(2.0))) - 13.0


def top_of(value):
    by_row = jnp.max(jnp.abs(value), axis=1, keepdims=True)
    return jnp.max(by_row, axis=0, keepdims=True)


def above(place, core, step, n_mp):
    return lax.rem(place[2] + n_mp + (1 - 2 * core) * step, n_mp)


def row_at(index, size):
    return pl.multiple_of(index * size, size)


def lay_kernel(*refs):
    models, out = refs[:-1], refs[-1]
    count = out.shape[0] // 4
    if len(models) == 1:
        wholes = [models[0][:, side, :] for side in range(2)]
    else:
        wholes = [jnp.concatenate([m[:, 0, :], m[:, 1, :]], axis=1) for m in models]
    for core, whole in enumerate(wholes):
        for d in range(count):
            out[core * count + d] = whole
            out[(2 + core) * count + d] = whole


def prepare_kernel(place, scales, latent, noise, embed, normed, stream, scaled, *, piece):
    rows = latent[place[1]].astype(F32)
    normed[...] = normalize(rows + embed[...])
    half = rows.shape[0] // 2
    for core in range(2):
        at = pl.multiple_of(core * half + place[2] * piece, piece)
        to = slice(core * piece, (core + 1) * piece)
        stream[to, :] = latent[place[1], pl.ds(at, piece), :].astype(F32)
        scaled[to, :] = scales[1] * noise[place[1], pl.ds(at, piece), :].astype(F32)


def gen_rows(place, core, piece, n_mp):
    half = n_mp * piece
    for k in range(1, n_mp // 2):
        for owner in range(2):
            yield pl.multiple_of(owner * half + above(place, core, k, n_mp) * piece, piece)
    for k in (0, n_mp // 2):
        yield pl.multiple_of(core * half + above(place, core, k, n_mp) * piece, piece)


def gen_kernel(place, normed, mine, other, *refs):
    preact_ref, active_ref, own, across = refs[:4]
    blocks, rows_of = refs[4:-1], refs[-1]
    piece = own.shape[0]
    n_mp = rows_of.shape[0] // piece
    for i, at in enumerate(gen_rows(place, place[0], piece, n_mp)):
        rows_of[i * piece : (i + 1) * piece, :] = normed[pl.ds(at, piece), :]

    def run(w_in, w_out):
        preact, active, partial = forward_part(rows_of[...], w_in[...], w_out[...])
        preact_ref[...] = preact
        active_ref[...] = active
        for k, block in enumerate(blocks):
            block[...] = partial[2 * k * piece : 2 * (k + 1) * piece, :]
        at = 2 * len(blocks) * piece
        own[...] = partial[at : at + piece, :]
        across[...] = partial[at + piece :, :]

    on_core(place, run, mine, other)


def sums_kernel(place, own, across, *refs):
    blocks, out = refs[:-1], refs[-1]
    piece = own.shape[0]
    total = 0.0
    for block in blocks:
        total = total + block[...].astype(F32)
    out[...] = total
    at = pl.ds(row_at(place[0], piece), piece)
    out[at, :] = out[at, :] + (own[...].astype(F32) + across[...].astype(F32))


def latent_kernel(place, scales, sums, came, stream, scaled, latents, noised, mine):
    piece = mine.shape[0]
    latents[...] = stream[...] + (sums[...] + came[...])
    noised[...] = (scales[0] * latents[...] + scaled[...]).astype(BF16)
    mine[...] = noised[pl.ds(row_at(place[0], piece), piece), :]


def order_kernel(*refs):
    blocks, out = refs[:-1], refs[-1]
    at = 0
    for block in blocks:
        out[at : at + block.shape[0], :] = block[...]
        at += block.shape[0]


def rows_in_order(place, own, came, pair, store):
    piece = pair.shape[0] // 2
    n_mp = (own.shape[0] // piece + 1) // 2 * 2
    half = n_mp * piece

    def at(core, z):
        return pl.multiple_of(core * half + z * piece, piece)

    for core in range(2):
        store(at(core, place[2]), pair[core * piece : (core + 1) * piece, :])
    for source, sender in ((own, place[0]), (came, 1 - place[0])):
        for k in range(1, n_mp // 2):
            z = above(place, sender, -k, n_mp)
            for core in range(2):
                to = ((k - 1) * 2 + core) * piece
                store(at(core, z), source[to : to + piece, :])
        to = (n_mp - 2) * piece
        store(at(sender, above(place, sender, n_mp // 2, n_mp)), source[to : to + piece, :])


def score_kernel(place, pair, own, came, embed, weights, out, both):
    n_mp, piece = out.shape[0], out.shape[1] // 2
    width = embed.shape[1]
    half = n_mp * piece
    rows = 2 * half
    hidden = weights.shape[1] // 2

    def store(at, value):
        summed = value.astype(F32)
        both[pl.ds(at, piece), :] = normalize(summed + embed[...])
        both[pl.ds(pl.multiple_of(rows + at, piece), piece), :] = normalize(summed)

    rows_in_order(place, own, came, pair, store)

    def finish(value):
        power = power_of(top_of(value))
        value = value * jnp.exp2(-power)
        tail = jnp.broadcast_to(power, (2 * piece, LANES))
        for j in range(n_mp):
            for h in range(2):
                at = h * half + j * piece
                out[j, h * piece : (h + 1) * piece, :width] = value[at : at + piece, :]
            out[j, :, width:] = tail

    @pl.when(place[0] == 0)
    def _():
        fake = forward_part(both[:rows, :], weights[:, :hidden], weights[:, hidden:])[2]
        finish(fake.astype(F32))

    @pl.when(place[0] != 0)
    def _():
        real = forward_part(both[...], weights[:, :hidden], weights[:, hidden:])[2]
        uncond, cond = real[rows:].astype(F32), real[:rows].astype(F32)
        finish(uncond + GUIDANCE * (cond - uncond))


def refresh_kernel(place, pair, own, came, *refs):
    embed, weights, normed_gen, active_own, active_came, preact_own, preact_came = refs[-10:-3]
    normed, preact, active = refs[-3:]
    piece = pair.shape[0] // 2
    n_mp = normed.shape[0] // (2 * piece)
    hidden = preact.shape[1]

    def store(at, value):
        normed[pl.ds(at, piece), :] = normalize(value.astype(F32) + embed[...])

    @pl.when(place[0] == 0)
    def _():
        rows_in_order(place, own, came, pair, store)
        preact[...] = jnp.dot(normed[...], weights[:, :hidden], preferred_element_type=F32)
        active[...] = jax.nn.gelu(preact[...]).astype(BF16)

    @pl.when(place[0] != 0)
    def _():
        normed[...] = normed_gen[...]
        for core, acts, pres in ((1, active_own, preact_own), (0, active_came, preact_came)):
            for i, at in enumerate(gen_rows(place, core, piece, n_mp)):
                active[pl.ds(at, piece), :] = acts[i * piece : (i + 1) * piece, :]
                preact[pl.ds(at, piece), :] = pres[i * piece : (i + 1) * piece, :]


def total_kernel(blocks, out):
    width = out.shape[1]
    total = 0.0
    for j in range(blocks.shape[0]):
        total = total + blocks[j, :, :width] * jnp.exp2(blocks[j, 0:1, width : width + 1])
    out[...] = total


def pack_kernel(place, own, other, latents_ref, noised, out, *, loss_scale):
    width = own.shape[1]
    piece = own.shape[0] // 2
    first = place[0] == 0

    def run(fake_sum, real_sum):
        latents = latents_ref[...]
        base = noised[...].astype(F32)
        fake = base + fake_sum[...]
        real_mix = base + real_sum[...]
        away = jnp.sum(jnp.abs(latents - real_mix), axis=1, keepdims=True)
        gap = jnp.sum(away, axis=0, keepdims=True)
        fake_delta = (2.0 * (fake - latents) * loss_scale).astype(BF16).astype(F32)
        value = jnp.where(first, fake_delta, fake - real_mix)
        power = power_of(top_of(value))
        out[:, :width] = value * jnp.exp2(-power)
        gap_power = power_of(gap)
        scaled = gap * jnp.exp2(-gap_power)
        coarse = jnp.floor(scaled * (1.0 / 16.0)) * 16.0
        line = lax.broadcasted_iota(jnp.int32, (2 * piece, LANES), 0)
        tail = jnp.where(line == 8, gap_power, power)
        tail = jnp.where(line == 9, coarse, tail)
        out[:, width:] = jnp.where(line == 10, scaled - coarse, tail)

    pl.when(first)(lambda: run(own, other))
    pl.when(place[0] != 0)(lambda: run(other, own))


def grad_kernel(
    place, blocks, weights, slope, normed, active, out, delta, grads, *, loss_scale, count, row_piece
):
    n_mp, piece = blocks.shape[0], blocks.shape[1] // 2
    rows, width = normed.shape
    hidden = active.shape[1]
    half = rows // 2
    gap = 0.0
    for j in range(n_mp):
        tail = blocks[j, :, width:]
        gap = gap + (tail[9:10, 0:1] + tail[10:11, 0:1]) * jnp.exp2(tail[8:9, 0:1])
    first = place[0] == 0
    weight = jnp.where(first, 1.0, 1.0 / (gap / count + MEAN_EPS))
    scale = jnp.where(first, 1.0, loss_scale)
    for j in range(n_mp):
        value = blocks[j, :, :width] * jnp.exp2(blocks[j, 0:1, width : width + 1])
        value = (value * weight * scale).astype(BF16)
        for h in range(2):
            at = h * half + j * piece
            delta[at : at + piece, :] = value[h * piece : (h + 1) * piece, :]
    size = row_piece * hidden // LANES
    chunk = row_piece * 8
    turned = delta[...].T
    powers = []

    def outer(side, turned, right):
        highest = jnp.zeros((8, LANES), F32)
        for c in range(width // chunk):
            block = jnp.dot(
                turned[c * chunk : (c + 1) * chunk, :], right, preferred_element_type=F32
            )
            grads[c * chunk : (c + 1) * chunk, :] = block
            for t in range(hidden // LANES):
                lanes = jnp.abs(block[:, t * LANES : (t + 1) * LANES]).reshape(-1, 8, LANES)
                highest = jnp.maximum(highest, jnp.max(lanes, axis=0))
        power = power_of(top_of(highest))
        factor = jnp.exp2(-power)
        for owner, (slot, part) in enumerate(SLOTS):
            for t in range(hidden // LANES):
                to = (part * 2 + side) * size + t * row_piece
                out[slot, to : to + row_piece, :] = (
                    grads[
                        owner * row_piece : (owner + 1) * row_piece,
                        t * LANES : (t + 1) * LANES,
                    ]
                    * factor
                )
        powers.append(power)

    outer(1, turned, active[...])
    back = jnp.dot(delta[...], weights[...], preferred_element_type=F32)
    outer(0, normed[...].T, (back * slope[...]).astype(BF16))
    line = lax.broadcasted_iota(jnp.int32, (16, LANES), 0)
    tail = jnp.where(line < 8, powers[1], powers[0])
    for d in range(out.shape[0]):
        out[d, 4 * size :, :] = tail


def collect_kernel(place, came, own, away):
    sources = came.shape[0]
    size = (came.shape[1] - 16) // 4
    for side in range(2):
        factors = [
            jnp.exp2(came[i, 4 * size + 8 * side : 4 * size + 8 * side + 1, 0:1])
            for i in range(sources)
        ]
        for out, core in ((own, place[0]), (away, 1 - place[0])):
            at = pl.multiple_of((core * 2 + side) * size, 8)
            total = came[0, pl.ds(at, size), :] * factors[0]
            for i in range(1, sources):
                total = total + came[i, pl.ds(at, size), :] * factors[i]
            out[side * size : (side + 1) * size, :] = total


def place_kernel(place, own, came, *outs):
    rows = outs[0].shape[0]
    tiles = outs[0].shape[2] // LANES

    def run(sources):
        for out, ref in zip(outs, sources):
            for side in range(2):
                for t in range(tiles):
                    at = (side * tiles + t) * rows
                    out[:, side, t * LANES : (t + 1) * LANES] = ref[at : at + rows, :]

    pl.when(place[0] == 0)(lambda: run((own, came)))
    pl.when(place[0] != 0)(lambda: run((came, own)))


def local(
    latent_noise,
    score_noise,
    timesteps,
    classes,
    class_table,
    gen_weights,
    real_weights,
    fake_weights,
):
    group_index = lax.axis_index("group")
    core = group_index % 2
    y_lo = group_index // 2
    n_dp = lax.axis_size("dp")
    n_mp = lax.axis_size("mp")
    samples, positions, width = latent_noise.shape
    rows = positions // 2
    piece = rows // n_mp
    row_piece, _, hidden = gen_weights.shape
    loss_scale = 1.0 / math.sqrt(samples * n_dp * positions)
    place = jnp.stack([core, y_lo, lax.axis_index("mp")]).astype(jnp.int32)
    work = 2 * rows * width * hidden

    def outgoing(models):
        lanes = hidden * len(models)
        blocks = [shape((4 * n_dp, row_piece, lanes), BF16)]
        return call(lay_kernel, "lay", models, [], blocks)[0]

    def gather(blocks):
        return lax.all_to_all(blocks, PLANE, 0, 0, tiled=True).reshape(width, -1)

    own_class = lax.dynamic_index_in_dim(classes, y_lo, keepdims=False)
    embedding = lax.dynamic_index_in_dim(class_table, own_class, keepdims=True).astype(F32)
    own_step = lax.dynamic_index_in_dim(timesteps, y_lo, keepdims=False)
    phase_angle = 0.5 * jnp.pi / TSTEPS * own_step.astype(F32)
    scales = jnp.stack([jnp.cos(phase_angle), jnp.sin(phase_angle)])
    prepared = call(
        lambda *refs: prepare_kernel(*refs, piece=piece),
        "prepare",
        [latent_noise, score_noise, embedding],
        [place, scales],
        [
            shape((positions, width), BF16),
            shape((2 * piece, width), F32),
            shape((2 * piece, width), F32),
        ],
    )

    gen_mine, score_blocks, prepared, embedding, scales = lax.optimization_barrier(
        (
            gather(outgoing([gen_weights])),
            outgoing([fake_weights, real_weights]),
            prepared,
            embedding,
            scales,
        )
    )
    normed_gen, stream, scaled_noise = prepared
    score_weights = gather(score_blocks)
    gen_other = core_swap(gen_mine)

    steps = n_mp // 2 - 1
    one = shape((piece, width), BF16)
    two = shape((2 * piece, width), BF16)
    preact_gen, active_gen, own, across, *sent = call(
        gen_kernel,
        "generate",
        [normed_gen, gen_mine, gen_other],
        [place],
        [shape((rows, hidden), F32), shape((rows, hidden), BF16), one, one] + [two] * steps,
        2 * work,
        [pltpu.VMEM((rows, width), BF16)],
        room=60,
    )
    came = [paired(block, k + 1) for k, block in enumerate(sent)]
    across = paired(across, n_mp // 2)
    both_f32 = shape((2 * piece, width), F32)
    (sums,) = call(sums_kernel, "sums", [own, across] + came, [place], [both_f32])
    latents, noised, noised_mine = call(
        latent_kernel,
        "latent",
        [sums, core_swap(sums), stream, scaled_noise],
        [place, scales],
        [both_f32, two, one],
    )
    around = [paired(noised, k + 1) for k in range(steps)]
    around.append(paired(noised_mine, n_mp // 2))
    (around,) = call(
        order_kernel, "order", around, [], [shape(((2 * steps + 1) * piece, width), BF16)]
    )
    around_other = core_swap(around)
    score_weights, around_other = lax.optimization_barrier((score_weights, around_other))
    (score_parts,) = call(
        score_kernel,
        "score",
        [noised, around, around_other, embedding, score_weights],
        [place],
        [shape((n_mp, 2 * piece, width + LANES), F32)],
        8 * work,
        [pltpu.VMEM((2 * positions, width), BF16)],
    )

    def exchange(blocks):
        return lax.all_to_all(blocks.astype(jnp.float16), "mp", 0, 0, tiled=True).astype(F32)

    (total,) = call(
        total_kernel, "total", [exchange(score_parts)], [], [shape((2 * piece, width), F32)]
    )
    (message,) = call(
        lambda *refs: pack_kernel(*refs, loss_scale=loss_scale),
        "pack",
        [total, core_swap(total), latents, noised],
        [place],
        [shape((2 * piece, width + LANES), F32)],
    )

    message, around, around_other = lax.optimization_barrier((message, around, around_other))
    normed, preact, active = call(
        refresh_kernel,
        "refresh",
        [noised, around, around_other, embedding, score_weights, normed_gen]
        + [active_gen, core_swap(active_gen), preact_gen, core_swap(preact_gen)],
        [place],
        [
            shape((positions, width), BF16),
            shape((positions, hidden), F32),
            shape((positions, hidden), BF16),
        ],
        2 * work,
    )
    slope = jax.vjp(jax.nn.gelu, preact)[1](jnp.ones_like(preact))[0]
    size = row_piece * hidden // LANES
    (grads,) = call(
        lambda *refs: grad_kernel(
            *refs, loss_scale=loss_scale, count=positions * width, row_piece=row_piece
        ),
        "grads",
        [
            exchange(jnp.broadcast_to(message[None], (n_mp,) + message.shape)),
            jnp.where(core == 0, score_weights[:, hidden:], gen_mine),
            slope,
            normed,
            active,
        ],
        [place],
        [shape((len(WALK), 4 * size + 16, LANES), F32)],
        6 * work,
        [pltpu.VMEM((positions, width), BF16), pltpu.VMEM((width, hidden), F32)],
    )
    came = lax.all_to_all(
        grads.astype(jnp.float16), PLANE, 0, 0, axis_index_groups=PEERS, tiled=True
    )
    own, away = call(
        collect_kernel,
        "collect",
        [came.astype(F32)],
        [place],
        [shape((2 * size, LANES), F32)] * 2,
    )
    fake_grad, gen_grad = call(
        place_kernel,
        "place",
        [own, core_swap(away)],
        [place],
        [shape((row_piece, 2, hidden), F32)] * 2,
    )
    return (gen_grad, fake_grad)


def solution(mesh):
    return jax.shard_map(
        local,
        mesh=mesh,
        in_specs=(
            P("dp", None, None),
            P("dp", None, None),
            P("dp"),
            P("dp"),
            P(),
            P(("group", "dp"), None, "mp"),
            P(("group", "dp"), None, "mp"),
            P(("group", "dp"), None, "mp"),
        ),
        out_specs=(P(("group", "dp"), None, "mp"), P(("group", "dp"), None, "mp")),
        check_vma=False,
    )
```

```python
import math

import jax
import jax.numpy as jnp
from jax import lax
from jax.experimental import pallas as pl
from jax.experimental.pallas import tpu as pltpu
from jax.sharding import PartitionSpec as P

TSTEPS = 1000
GUIDANCE = 3.0
EPSILON = 1e-06
MEAN_EPS = 1e-05

PLANE = ("group", "dp")
LANES = 128
WALK = [(0, 0), (1, 0), (2, 0), (3, 0), (3, 1), (2, 1), (1, 1), (1, 2)]
WALK += [(2, 2), (3, 2), (3, 3), (2, 3), (1, 3), (0, 3), (0, 2), (0, 1)]
SLOTS = [
    (WALK.index((x, y_hi * 2 + y_lo)), core)
    for y_lo in range(2)
    for core in range(2)
    for x in range(4)
    for y_hi in range(2)
]
PEERS = [[((y % 2) * 2 + core) * 8 + x * 2 + y // 2 for x, y in WALK] for core in range(2)]
SMEM = pl.BlockSpec(memory_space=pltpu.SMEM)
VMEM = pl.BlockSpec(memory_space=pltpu.VMEM)
HBM = pl.BlockSpec(memory_space=pltpu.HBM)
F32 = jnp.float32
BF16 = jnp.bfloat16


def call(body, name, inputs, scalars, outs, flops=0, scratch=(), room=40, far=()):
    arrays = list(inputs) + list(far)
    moved = sum(math.prod(a.shape) * a.dtype.itemsize for a in arrays + list(outs))
    return pl.pallas_call(
        body,
        name=name,
        out_shape=outs,
        in_specs=[SMEM] * len(scalars) + [VMEM] * len(inputs) + [HBM] * len(far),
        out_specs=[VMEM] * len(outs),
        scratch_shapes=list(scratch),
        compiler_params=pltpu.CompilerParams(vmem_limit_bytes=room * 2**20),
        cost_estimate=pl.CostEstimate(flops=flops, bytes_accessed=moved, transcendentals=0),
    )(*scalars, *arrays)


def shape(dims, dtype):
    return jax.ShapeDtypeStruct(dims, dtype)


def normalize(summed):
    factor = lax.rsqrt(jnp.mean(summed * summed, axis=-1, keepdims=True) + EPSILON)
    return (summed * factor).astype(BF16)


def dot_t(left, right):
    return lax.dot_general(left, right, (((1,), (1,)), ((), ())), preferred_element_type=F32)


def forward_part(normed, w_in, w_out):
    preact = jnp.dot(normed, w_in, preferred_element_type=F32)
    active = jax.nn.gelu(preact).astype(BF16)
    return preact, active, dot_t(active, w_out).astype(BF16)


def core_swap(block):
    return lax.ppermute(block, "group", [(0, 1), (1, 0), (2, 3), (3, 2)])


def paired(block, step):
    n_mp = lax.axis_size("mp")
    pairs = []
    for group in range(lax.axis_size("group")):
        sign = 1 - 2 * (group % 2)
        for z in range(n_mp):
            pairs.append((group * n_mp + z, group * n_mp + (z + sign * step) % n_mp))
    return lax.ppermute(block, ("group", "mp"), pairs)


def on_core(place, run, mine, other):
    pl.when(place[0] == 0)(lambda: run(mine, other))
    pl.when(place[0] != 0)(lambda: run(other, mine))


def power_of(peak):
    return jnp.floor(jnp.log(jnp.maximum(peak, 1e-30)) * (1.0 / math.log(2.0))) - 13.0


def top_of(value):
    by_row = jnp.max(jnp.abs(value), axis=1, keepdims=True)
    return jnp.max(by_row, axis=0, keepdims=True)


def above(place, core, step, n_mp):
    return lax.rem(place[2] + n_mp + (1 - 2 * core) * step, n_mp)


def row_at(index, size):
    return pl.multiple_of(index * size, size)


def lay_kernel(*refs):
    models, out = refs[:-1], refs[-1]
    count = out.shape[0] // 4
    if len(models) == 1:
        wholes = [models[0][:, side, :] for side in range(2)]
    else:
        wholes = [jnp.concatenate([m[:, 0, :], m[:, 1, :]], axis=1) for m in models]
    for core, whole in enumerate(wholes):
        for d in range(count):
            out[core * count + d] = whole
            out[(2 + core) * count + d] = whole


def prepare_kernel(place, scales, latent, noise, embed, normed, stream, scaled, *, piece):
    rows = latent[place[1]].astype(F32)
    normed[...] = normalize(rows + embed[...])
    half = rows.shape[0] // 2
    for core in range(2):
        at = pl.multiple_of(core * half + place[2] * piece, piece)
        to = slice(core * piece, (core + 1) * piece)
        stream[to, :] = latent[place[1], pl.ds(at, piece), :].astype(F32)
        scaled[to, :] = scales[1] * noise[place[1], pl.ds(at, piece), :].astype(F32)


def gen_rows(place, core, piece, n_mp):
    half = n_mp * piece
    for k in range(1, n_mp // 2):
        for owner in range(2):
            yield pl.multiple_of(owner * half + above(place, core, k, n_mp) * piece, piece)
    for k in (0, n_mp // 2):
        yield pl.multiple_of(core * half + above(place, core, k, n_mp) * piece, piece)


def gen_kernel(place, normed, mine, other, *refs):
    preact_ref, active_ref, own, across = refs[:4]
    blocks, rows_of = refs[4:-1], refs[-1]
    piece = own.shape[0]
    n_mp = rows_of.shape[0] // piece
    for i, at in enumerate(gen_rows(place, place[0], piece, n_mp)):
        rows_of[i * piece : (i + 1) * piece, :] = normed[pl.ds(at, piece), :]

    def run(w_in, w_out):
        preact, active, partial = forward_part(rows_of[...], w_in[...], w_out[...])
        preact_ref[...] = preact
        active_ref[...] = active
        for k, block in enumerate(blocks):
            block[...] = partial[2 * k * piece : 2 * (k + 1) * piece, :]
        at = 2 * len(blocks) * piece
        own[...] = partial[at : at + piece, :]
        across[...] = partial[at + piece :, :]

    on_core(place, run, mine, other)


def sums_kernel(place, own, across, *refs):
    blocks, out = refs[:-1], refs[-1]
    piece = own.shape[0]
    total = 0.0
    for block in blocks:
        total = total + block[...].astype(F32)
    out[...] = total
    at = pl.ds(row_at(place[0], piece), piece)
    out[at, :] = out[at, :] + (own[...].astype(F32) + across[...].astype(F32))


def latent_kernel(place, scales, sums, came, stream, scaled, latents, noised, mine):
    piece = mine.shape[0]
    latents[...] = stream[...] + (sums[...] + came[...])
    noised[...] = (scales[0] * latents[...] + scaled[...]).astype(BF16)
    mine[...] = noised[pl.ds(row_at(place[0], piece), piece), :]


def order_kernel(*refs):
    blocks, out = refs[:-1], refs[-1]
    at = 0
    for block in blocks:
        out[at : at + block.shape[0], :] = block[...]
        at += block.shape[0]


def rows_in_order(place, own, came, pair, store):
    piece = pair.shape[0] // 2
    n_mp = (own.shape[0] // piece + 1) // 2 * 2
    half = n_mp * piece

    def at(core, z):
        return pl.multiple_of(core * half + z * piece, piece)

    for core in range(2):
        store(at(core, place[2]), pair[core * piece : (core + 1) * piece, :])
    for source, sender in ((own, place[0]), (came, 1 - place[0])):
        for k in range(1, n_mp // 2):
            z = above(place, sender, -k, n_mp)
            for core in range(2):
                to = ((k - 1) * 2 + core) * piece
                store(at(core, z), source[to : to + piece, :])
        to = (n_mp - 2) * piece
        store(at(sender, above(place, sender, n_mp // 2, n_mp)), source[to : to + piece, :])


def score_kernel(place, pair, own, came, embed, weights, out, both, w_in, w_out, sems):
    n_mp, piece = out.shape[0], out.shape[1] // 2
    width = embed.shape[1]
    half = n_mp * piece
    rows = 2 * half
    hidden = w_in.shape[1]
    copies = [
        pltpu.make_async_copy(weights.at[:, pl.ds(i * hidden, hidden)], target, sems.at[i])
        for i, target in enumerate((w_in, w_out))
    ]
    for copy in copies:
        copy.start()

    def store(at, value):
        summed = value.astype(F32)
        both[pl.ds(at, piece), :] = normalize(summed + embed[...])
        both[pl.ds(pl.multiple_of(rows + at, piece), piece), :] = normalize(summed)

    rows_in_order(place, own, came, pair, store)
    for copy in copies:
        copy.wait()

    def finish(value):
        power = power_of(top_of(value))
        value = value * jnp.exp2(-power)
        tail = jnp.broadcast_to(power, (2 * piece, LANES))
        for j in range(n_mp):
            for h in range(2):
                at = h * half + j * piece
                out[j, h * piece : (h + 1) * piece, :width] = value[at : at + piece, :]
            out[j, :, width:] = tail

    @pl.when(place[0] == 0)
    def _():
        fake = forward_part(both[:rows, :], w_in[...], w_out[...])[2]
        finish(fake.astype(F32))

    @pl.when(place[0] != 0)
    def _():
        real = forward_part(both[...], w_in[...], w_out[...])[2]
        uncond, cond = real[rows:].astype(F32), real[:rows].astype(F32)
        finish(uncond + GUIDANCE * (cond - uncond))


def refresh_kernel(place, pair, own, came, *refs):
    embed, weights, normed_gen, active_own, active_came, preact_own, preact_came = refs[-10:-3]
    normed, preact, active = refs[-3:]
    piece = pair.shape[0] // 2
    n_mp = normed.shape[0] // (2 * piece)
    hidden = preact.shape[1]

    def store(at, value):
        normed[pl.ds(at, piece), :] = normalize(value.astype(F32) + embed[...])

    @pl.when(place[0] == 0)
    def _():
        rows_in_order(place, own, came, pair, store)
        preact[...] = jnp.dot(normed[...], weights[:, :hidden], preferred_element_type=F32)
        active[...] = jax.nn.gelu(preact[...]).astype(BF16)

    @pl.when(place[0] != 0)
    def _():
        normed[...] = normed_gen[...]
        for core, acts, pres in ((1, active_own, preact_own), (0, active_came, preact_came)):
            for i, at in enumerate(gen_rows(place, core, piece, n_mp)):
                active[pl.ds(at, piece), :] = acts[i * piece : (i + 1) * piece, :]
                preact[pl.ds(at, piece), :] = pres[i * piece : (i + 1) * piece, :]


def total_kernel(blocks, out):
    width = out.shape[1]
    total = 0.0
    for j in range(blocks.shape[0]):
        total = total + blocks[j, :, :width] * jnp.exp2(blocks[j, 0:1, width : width + 1])
    out[...] = total


def pack_kernel(place, own, other, latents_ref, noised, out, *, loss_scale):
    width = own.shape[1]
    piece = own.shape[0] // 2
    first = place[0] == 0

    def run(fake_sum, real_sum):
        latents = latents_ref[...]
        base = noised[...].astype(F32)
        fake = base + fake_sum[...]
        real_mix = base + real_sum[...]
        away = jnp.sum(jnp.abs(latents - real_mix), axis=1, keepdims=True)
        gap = jnp.sum(away, axis=0, keepdims=True)
        fake_delta = (2.0 * (fake - latents) * loss_scale).astype(BF16).astype(F32)
        value = jnp.where(first, fake_delta, fake - real_mix)
        power = power_of(top_of(value))
        out[:, :width] = value * jnp.exp2(-power)
        gap_power = power_of(gap)
        scaled = gap * jnp.exp2(-gap_power)
        coarse = jnp.floor(scaled * (1.0 / 16.0)) * 16.0
        line = lax.broadcasted_iota(jnp.int32, (2 * piece, LANES), 0)
        tail = jnp.where(line == 8, gap_power, power)
        tail = jnp.where(line == 9, coarse, tail)
        out[:, width:] = jnp.where(line == 10, scaled - coarse, tail)

    pl.when(first)(lambda: run(own, other))
    pl.when(place[0] != 0)(lambda: run(other, own))


def grad_kernel(
    place, blocks, weights, slope, normed, active, out, delta, grads, *, loss_scale, count, row_piece
):
    n_mp, piece = blocks.shape[0], blocks.shape[1] // 2
    rows, width = normed.shape
    hidden = active.shape[1]
    half = rows // 2
    gap = 0.0
    for j in range(n_mp):
        tail = blocks[j, :, width:]
        gap = gap + (tail[9:10, 0:1] + tail[10:11, 0:1]) * jnp.exp2(tail[8:9, 0:1])
    first = place[0] == 0
    weight = jnp.where(first, 1.0, 1.0 / (gap / count + MEAN_EPS))
    scale = jnp.where(first, 1.0, loss_scale)
    for j in range(n_mp):
        value = blocks[j, :, :width] * jnp.exp2(blocks[j, 0:1, width : width + 1])
        value = (value * weight * scale).astype(BF16)
        for h in range(2):
            at = h * half + j * piece
            delta[at : at + piece, :] = value[h * piece : (h + 1) * piece, :]
    size = row_piece * hidden // LANES
    chunk = row_piece * 8
    turned = delta[...].T
    powers = []

    def outer(side, turned, right):
        highest = jnp.zeros((8, LANES), F32)
        for c in range(width // chunk):
            block = jnp.dot(
                turned[c * chunk : (c + 1) * chunk, :], right, preferred_element_type=F32
            )
            grads[c * chunk : (c + 1) * chunk, :] = block
            for t in range(hidden // LANES):
                lanes = jnp.abs(block[:, t * LANES : (t + 1) * LANES]).reshape(-1, 8, LANES)
                highest = jnp.maximum(highest, jnp.max(lanes, axis=0))
        power = power_of(top_of(highest))
        factor = jnp.exp2(-power)
        for owner, (slot, part) in enumerate(SLOTS):
            for t in range(hidden // LANES):
                to = (part * 2 + side) * size + t * row_piece
                out[slot, to : to + row_piece, :] = (
                    grads[
                        owner * row_piece : (owner + 1) * row_piece,
                        t * LANES : (t + 1) * LANES,
                    ]
                    * factor
                )
        powers.append(power)

    outer(1, turned, active[...])
    back = jnp.dot(delta[...], weights[...], preferred_element_type=F32)
    outer(0, normed[...].T, (back * slope[...]).astype(BF16))
    line = lax.broadcasted_iota(jnp.int32, (16, LANES), 0)
    tail = jnp.where(line < 8, powers[1], powers[0])
    for d in range(out.shape[0]):
        out[d, 4 * size :, :] = tail


def collect_kernel(place, came, own, away):
    sources = came.shape[0]
    size = (came.shape[1] - 16) // 4
    for side in range(2):
        factors = [
            jnp.exp2(came[i, 4 * size + 8 * side : 4 * size + 8 * side + 1, 0:1])
            for i in range(sources)
        ]
        for out, core in ((own, place[0]), (away, 1 - place[0])):
            at = pl.multiple_of((core * 2 + side) * size, 8)
            total = came[0, pl.ds(at, size), :] * factors[0]
            for i in range(1, sources):
                total = total + came[i, pl.ds(at, size), :] * factors[i]
            out[side * size : (side + 1) * size, :] = total


def place_kernel(place, own, came, *outs):
    rows = outs[0].shape[0]
    tiles = outs[0].shape[2] // LANES

    def run(sources):
        for out, ref in zip(outs, sources):
            for side in range(2):
                for t in range(tiles):
                    at = (side * tiles + t) * rows
                    out[:, side, t * LANES : (t + 1) * LANES] = ref[at : at + rows, :]

    pl.when(place[0] == 0)(lambda: run((own, came)))
    pl.when(place[0] != 0)(lambda: run((came, own)))


def local(
    latent_noise,
    score_noise,
    timesteps,
    classes,
    class_table,
    gen_weights,
    real_weights,
    fake_weights,
):
    group_index = lax.axis_index("group")
    core = group_index % 2
    y_lo = group_index // 2
    n_dp = lax.axis_size("dp")
    n_mp = lax.axis_size("mp")
    samples, positions, width = latent_noise.shape
    rows = positions // 2
    piece = rows // n_mp
    row_piece, _, hidden = gen_weights.shape
    loss_scale = 1.0 / math.sqrt(samples * n_dp * positions)
    place = jnp.stack([core, y_lo, lax.axis_index("mp")]).astype(jnp.int32)
    work = 2 * rows * width * hidden

    def outgoing(models):
        lanes = hidden * len(models)
        blocks = [shape((4 * n_dp, row_piece, lanes), BF16)]
        return call(lay_kernel, "lay", models, [], blocks)[0]

    def gather(blocks):
        return lax.all_to_all(blocks, PLANE, 0, 0, tiled=True).reshape(width, -1)

    own_class = lax.dynamic_index_in_dim(classes, y_lo, keepdims=False)
    embedding = lax.dynamic_index_in_dim(class_table, own_class, keepdims=True).astype(F32)
    own_step = lax.dynamic_index_in_dim(timesteps, y_lo, keepdims=False)
    phase_angle = 0.5 * jnp.pi / TSTEPS * own_step.astype(F32)
    scales = jnp.stack([jnp.cos(phase_angle), jnp.sin(phase_angle)])
    prepared = call(
        lambda *refs: prepare_kernel(*refs, piece=piece),
        "prepare",
        [latent_noise, score_noise, embedding],
        [place, scales],
        [
            shape((positions, width), BF16),
            shape((2 * piece, width), F32),
            shape((2 * piece, width), F32),
        ],
    )

    gen_mine, score_blocks, prepared, embedding, scales = lax.optimization_barrier(
        (
            gather(outgoing([gen_weights])),
            outgoing([fake_weights, real_weights]),
            prepared,
            embedding,
            scales,
        )
    )
    normed_gen, stream, scaled_noise = prepared
    score_weights = gather(score_blocks)
    gen_other = core_swap(gen_mine)

    steps = n_mp // 2 - 1
    one = shape((piece, width), BF16)
    two = shape((2 * piece, width), BF16)
    preact_gen, active_gen, own, across, *sent = call(
        gen_kernel,
        "generate",
        [normed_gen, gen_mine, gen_other],
        [place],
        [shape((rows, hidden), F32), shape((rows, hidden), BF16), one, one] + [two] * steps,
        2 * work,
        [pltpu.VMEM((rows, width), BF16)],
        room=60,
    )
    came = [paired(block, k + 1) for k, block in enumerate(sent)]
    across = paired(across, n_mp // 2)
    both_f32 = shape((2 * piece, width), F32)
    (sums,) = call(sums_kernel, "sums", [own, across] + came, [place], [both_f32])
    latents, noised, noised_mine = call(
        latent_kernel,
        "latent",
        [sums, core_swap(sums), stream, scaled_noise],
        [place, scales],
        [both_f32, two, one],
    )
    around = [paired(noised, k + 1) for k in range(steps)]
    around.append(paired(noised_mine, n_mp // 2))
    (around,) = call(
        order_kernel, "order", around, [], [shape(((2 * steps + 1) * piece, width), BF16)]
    )
    around_other = core_swap(around)
    score_weights, around_other = lax.optimization_barrier((score_weights, around_other))
    (score_parts,) = call(
        score_kernel,
        "score",
        [noised, around, around_other, embedding],
        [place],
        [shape((n_mp, 2 * piece, width + LANES), F32)],
        8 * work,
        [pltpu.VMEM((2 * positions, width), BF16)]
        + [pltpu.VMEM((width, hidden), BF16)] * 2
        + [pltpu.SemaphoreType.DMA((2,))],
        room=60,
        far=[score_weights],
    )

    def exchange(blocks):
        return lax.all_to_all(blocks.astype(jnp.float16), "mp", 0, 0, tiled=True).astype(F32)

    (total,) = call(
        total_kernel, "total", [exchange(score_parts)], [], [shape((2 * piece, width), F32)]
    )
    (message,) = call(
        lambda *refs: pack_kernel(*refs, loss_scale=loss_scale),
        "pack",
        [total, core_swap(total), latents, noised],
        [place],
        [shape((2 * piece, width + LANES), F32)],
    )

    message, around, around_other = lax.optimization_barrier((message, around, around_other))
    normed, preact, active = call(
        refresh_kernel,
        "refresh",
        [noised, around, around_other, embedding, score_weights, normed_gen]
        + [active_gen, core_swap(active_gen), preact_gen, core_swap(preact_gen)],
        [place],
        [
            shape((positions, width), BF16),
            shape((positions, hidden), F32),
            shape((positions, hidden), BF16),
        ],
        2 * work,
    )
    slope = jax.vjp(jax.nn.gelu, preact)[1](jnp.ones_like(preact))[0]
    size = row_piece * hidden // LANES
    (grads,) = call(
        lambda *refs: grad_kernel(
            *refs, loss_scale=loss_scale, count=positions * width, row_piece=row_piece
        ),
        "grads",
        [
            exchange(jnp.broadcast_to(message[None], (n_mp,) + message.shape)),
            jnp.where(core == 0, score_weights[:, hidden:], gen_mine),
            slope,
            normed,
            active,
        ],
        [place],
        [shape((len(WALK), 4 * size + 16, LANES), F32)],
        6 * work,
        [pltpu.VMEM((positions, width), BF16), pltpu.VMEM((width, hidden), F32)],
    )
    came = lax.all_to_all(
        grads.astype(jnp.float16), PLANE, 0, 0, axis_index_groups=PEERS, tiled=True
    )
    own, away = call(
        collect_kernel,
        "collect",
        [came.astype(F32)],
        [place],
        [shape((2 * size, LANES), F32)] * 2,
    )
    fake_grad, gen_grad = call(
        place_kernel,
        "place",
        [own, core_swap(away)],
        [place],
        [shape((row_piece, 2, hidden), F32)] * 2,
    )
    return (gen_grad, fake_grad)


def solution(mesh):
    return jax.shard_map(
        local,
        mesh=mesh,
        in_specs=(
            P("dp", None, None),
            P("dp", None, None),
            P("dp"),
            P("dp"),
            P(),
            P(("group", "dp"), None, "mp"),
            P(("group", "dp"), None, "mp"),
            P(("group", "dp"), None, "mp"),
        ),
        out_specs=(P(("group", "dp"), None, "mp"), P(("group", "dp"), None, "mp")),
        check_vma=False,
    )
```

```python
import math

import jax
import jax.numpy as jnp
from jax import lax
from jax.experimental import pallas as pl
from jax.experimental.pallas import tpu as pltpu
from jax.sharding import PartitionSpec as P

TSTEPS = 1000
GUIDANCE = 3.0
EPSILON = 1e-06
MEAN_EPS = 1e-05

PLANE = ("group", "dp")
LANES = 128
WALK = [(0, 0), (1, 0), (2, 0), (3, 0), (3, 1), (2, 1), (1, 1), (1, 2)]
WALK += [(2, 2), (3, 2), (3, 3), (2, 3), (1, 3), (0, 3), (0, 2), (0, 1)]
SLOTS = [
    (WALK.index((x, y_hi * 2 + y_lo)), core)
    for y_lo in range(2)
    for core in range(2)
    for x in range(4)
    for y_hi in range(2)
]
PEERS = [[((y % 2) * 2 + core) * 8 + x * 2 + y // 2 for x, y in WALK] for core in range(2)]
SMEM = pl.BlockSpec(memory_space=pltpu.SMEM)
VMEM = pl.BlockSpec(memory_space=pltpu.VMEM)
F32 = jnp.float32
BF16 = jnp.bfloat16


def call(body, name, inputs, scalars, outs, flops=0, scratch=(), room=40):
    moved = sum(math.prod(a.shape) * a.dtype.itemsize for a in list(inputs) + list(outs))
    return pl.pallas_call(
        body,
        name=name,
        out_shape=outs,
        in_specs=[SMEM] * len(scalars) + [VMEM] * len(inputs),
        out_specs=[VMEM] * len(outs),
        scratch_shapes=list(scratch),
        compiler_params=pltpu.CompilerParams(vmem_limit_bytes=room * 2**20),
        cost_estimate=pl.CostEstimate(flops=flops, bytes_accessed=moved, transcendentals=0),
    )(*scalars, *inputs)


def shape(dims, dtype):
    return jax.ShapeDtypeStruct(dims, dtype)


def normalize(summed):
    factor = lax.rsqrt(jnp.mean(summed * summed, axis=-1, keepdims=True) + EPSILON)
    return (summed * factor).astype(BF16)


def dot_t(left, right):
    return lax.dot_general(left, right, (((1,), (1,)), ((), ())), preferred_element_type=F32)


def forward_part(normed, w_in, w_out):
    preact = jnp.dot(normed, w_in, preferred_element_type=F32)
    active = jax.nn.gelu(preact).astype(BF16)
    return preact, active, dot_t(active, w_out).astype(BF16)


def core_swap(block):
    return lax.ppermute(block, "group", [(0, 1), (1, 0), (2, 3), (3, 2)])


def paired(block, step):
    n_mp = lax.axis_size("mp")
    pairs = []
    for group in range(lax.axis_size("group")):
        sign = 1 - 2 * (group % 2)
        for z in range(n_mp):
            pairs.append((group * n_mp + z, group * n_mp + (z + sign * step) % n_mp))
    return lax.ppermute(block, ("group", "mp"), pairs)


def on_core(place, run, mine, other):
    pl.when(place[0] == 0)(lambda: run(mine, other))
    pl.when(place[0] != 0)(lambda: run(other, mine))


def power_of(peak):
    return jnp.floor(jnp.log(jnp.maximum(peak, 1e-30)) * (1.0 / math.log(2.0))) - 13.0


def top_of(value):
    by_row = jnp.max(jnp.abs(value), axis=1, keepdims=True)
    return jnp.max(by_row, axis=0, keepdims=True)


def above(place, core, step, n_mp):
    return lax.rem(place[2] + n_mp + (1 - 2 * core) * step, n_mp)


def row_at(index, size):
    return pl.multiple_of(index * size, size)


def lay_kernel(*refs):
    models, out = refs[:-1], refs[-1]
    count = out.shape[0] // 4
    if len(models) == 1:
        wholes = [models[0][:, side, :] for side in range(2)]
    else:
        wholes = [jnp.concatenate([m[:, 0, :], m[:, 1, :]], axis=1) for m in models]
    for core, whole in enumerate(wholes):
        for d in range(count):
            out[core * count + d] = whole
            out[(2 + core) * count + d] = whole


def prepare_kernel(place, scales, latent, noise, embed, normed, stream, scaled, *, piece):
    rows = latent[place[1]].astype(F32)
    normed[...] = normalize(rows + embed[...])
    half = rows.shape[0] // 2
    for core in range(2):
        at = pl.multiple_of(core * half + place[2] * piece, piece)
        to = slice(core * piece, (core + 1) * piece)
        stream[to, :] = latent[place[1], pl.ds(at, piece), :].astype(F32)
        scaled[to, :] = scales[1] * noise[place[1], pl.ds(at, piece), :].astype(F32)


def gen_rows(place, core, piece, n_mp):
    half = n_mp * piece
    for k in range(1, n_mp // 2):
        for owner in range(2):
            yield pl.multiple_of(owner * half + above(place, core, k, n_mp) * piece, piece)
    for k in (0, n_mp // 2):
        yield pl.multiple_of(core * half + above(place, core, k, n_mp) * piece, piece)


def gen_kernel(place, normed, mine, other, *refs):
    preact_ref, active_ref, own, across = refs[:4]
    blocks, rows_of = refs[4:-1], refs[-1]
    piece = own.shape[0]
    n_mp = rows_of.shape[0] // piece
    for i, at in enumerate(gen_rows(place, place[0], piece, n_mp)):
        rows_of[i * piece : (i + 1) * piece, :] = normed[pl.ds(at, piece), :]

    def run(w_in, w_out):
        preact, active, partial = forward_part(rows_of[...], w_in[...], w_out[...])
        preact_ref[...] = preact
        active_ref[...] = active
        for k, block in enumerate(blocks):
            block[...] = partial[2 * k * piece : 2 * (k + 1) * piece, :]
        at = 2 * len(blocks) * piece
        own[...] = partial[at : at + piece, :]
        across[...] = partial[at + piece :, :]

    on_core(place, run, mine, other)


def sums_kernel(place, own, across, *refs):
    blocks, out = refs[:-1], refs[-1]
    piece = own.shape[0]
    total = 0.0
    for block in blocks:
        total = total + block[...].astype(F32)
    out[...] = total
    at = pl.ds(row_at(place[0], piece), piece)
    out[at, :] = out[at, :] + (own[...].astype(F32) + across[...].astype(F32))


def latent_kernel(place, scales, sums, came, stream, scaled, latents, noised, mine):
    piece = mine.shape[0]
    latents[...] = stream[...] + (sums[...] + came[...])
    noised[...] = (scales[0] * latents[...] + scaled[...]).astype(BF16)
    mine[...] = noised[pl.ds(row_at(place[0], piece), piece), :]


def order_kernel(*refs):
    blocks, outs = refs[:-2], refs[-2:]
    at = 0
    for block in blocks:
        for out in outs:
            out[at : at + block.shape[0], :] = block[...]
        at += block.shape[0]


def rows_in_order(place, own, came, pair, store):
    piece = pair.shape[0] // 2
    n_mp = (own.shape[0] // piece + 1) // 2 * 2
    half = n_mp * piece

    def at(core, z):
        return pl.multiple_of(core * half + z * piece, piece)

    for core in range(2):
        store(at(core, place[2]), pair[core * piece : (core + 1) * piece, :])
    for source, sender in ((own, place[0]), (came, 1 - place[0])):
        for k in range(1, n_mp // 2):
            z = above(place, sender, -k, n_mp)
            for core in range(2):
                to = ((k - 1) * 2 + core) * piece
                store(at(core, z), source[to : to + piece, :])
        to = (n_mp - 2) * piece
        store(at(sender, above(place, sender, n_mp // 2, n_mp)), source[to : to + piece, :])


def score_kernel(place, pair, own, came, embed, weights, out, both):
    n_mp, piece = out.shape[0], out.shape[1] // 2
    width = embed.shape[1]
    half = n_mp * piece
    rows = 2 * half
    hidden = weights.shape[1] // 2

    def store(at, value):
        summed = value.astype(F32)
        both[pl.ds(at, piece), :] = normalize(summed + embed[...])
        both[pl.ds(pl.multiple_of(rows + at, piece), piece), :] = normalize(summed)

    rows_in_order(place, own, came, pair, store)

    def finish(value):
        power = power_of(top_of(value))
        value = value * jnp.exp2(-power)
        tail = jnp.broadcast_to(power, (2 * piece, LANES))
        for j in range(n_mp):
            for h in range(2):
                at = h * half + j * piece
                out[j, h * piece : (h + 1) * piece, :width] = value[at : at + piece, :]
            out[j, :, width:] = tail

    @pl.when(place[0] == 0)
    def _():
        fake = forward_part(both[:rows, :], weights[:, :hidden], weights[:, hidden:])[2]
        finish(fake.astype(F32))

    @pl.when(place[0] != 0)
    def _():
        real = forward_part(both[...], weights[:, :hidden], weights[:, hidden:])[2]
        uncond, cond = real[rows:].astype(F32), real[:rows].astype(F32)
        finish(uncond + GUIDANCE * (cond - uncond))


def refresh_kernel(place, pair, own, came, *refs):
    embed, weights, normed_gen, active_own, active_came, preact_own, preact_came = refs[-10:-3]
    normed, preact, active = refs[-3:]
    piece = pair.shape[0] // 2
    n_mp = normed.shape[0] // (2 * piece)
    hidden = preact.shape[1]

    def store(at, value):
        normed[pl.ds(at, piece), :] = normalize(value.astype(F32) + embed[...])

    @pl.when(place[0] == 0)
    def _():
        rows_in_order(place, own, came, pair, store)
        preact[...] = jnp.dot(normed[...], weights[:, :hidden], preferred_element_type=F32)
        active[...] = jax.nn.gelu(preact[...]).astype(BF16)

    @pl.when(place[0] != 0)
    def _():
        normed[...] = normed_gen[...]
        for core, acts, pres in ((1, active_own, preact_own), (0, active_came, preact_came)):
            for i, at in enumerate(gen_rows(place, core, piece, n_mp)):
                active[pl.ds(at, piece), :] = acts[i * piece : (i + 1) * piece, :]
                preact[pl.ds(at, piece), :] = pres[i * piece : (i + 1) * piece, :]


def total_kernel(blocks, out):
    width = out.shape[1]
    total = 0.0
    for j in range(blocks.shape[0]):
        total = total + blocks[j, :, :width] * jnp.exp2(blocks[j, 0:1, width : width + 1])
    out[...] = total


def pack_kernel(place, own, other, latents_ref, noised, out, *, loss_scale):
    width = own.shape[1]
    piece = own.shape[0] // 2
    first = place[0] == 0

    def run(fake_sum, real_sum):
        latents = latents_ref[...]
        base = noised[...].astype(F32)
        fake = base + fake_sum[...]
        real_mix = base + real_sum[...]
        away = jnp.sum(jnp.abs(latents - real_mix), axis=1, keepdims=True)
        gap = jnp.sum(away, axis=0, keepdims=True)
        fake_delta = (2.0 * (fake - latents) * loss_scale).astype(BF16).astype(F32)
        value = jnp.where(first, fake_delta, fake - real_mix)
        power = power_of(top_of(value))
        out[:, :width] = value * jnp.exp2(-power)
        gap_power = power_of(gap)
        scaled = gap * jnp.exp2(-gap_power)
        coarse = jnp.floor(scaled * (1.0 / 16.0)) * 16.0
        line = lax.broadcasted_iota(jnp.int32, (2 * piece, LANES), 0)
        tail = jnp.where(line == 8, gap_power, power)
        tail = jnp.where(line == 9, coarse, tail)
        out[:, width:] = jnp.where(line == 10, scaled - coarse, tail)

    pl.when(first)(lambda: run(own, other))
    pl.when(place[0] != 0)(lambda: run(other, own))


def grad_kernel(
    place, blocks, weights, slope, normed, active, out, delta, grads, *, loss_scale, count, row_piece
):
    n_mp, piece = blocks.shape[0], blocks.shape[1] // 2
    rows, width = normed.shape
    hidden = active.shape[1]
    half = rows // 2
    gap = 0.0
    for j in range(n_mp):
        tail = blocks[j, :, width:]
        gap = gap + (tail[9:10, 0:1] + tail[10:11, 0:1]) * jnp.exp2(tail[8:9, 0:1])
    first = place[0] == 0
    weight = jnp.where(first, 1.0, 1.0 / (gap / count + MEAN_EPS))
    scale = jnp.where(first, 1.0, loss_scale)
    for j in range(n_mp):
        value = blocks[j, :, :width] * jnp.exp2(blocks[j, 0:1, width : width + 1])
        value = (value * weight * scale).astype(BF16)
        for h in range(2):
            at = h * half + j * piece
            delta[at : at + piece, :] = value[h * piece : (h + 1) * piece, :]
    size = row_piece * hidden // LANES
    chunk = row_piece * 8
    turned = delta[...].T
    powers = []

    def outer(side, turned, right):
        highest = jnp.zeros((8, LANES), F32)
        for c in range(width // chunk):
            block = jnp.dot(
                turned[c * chunk : (c + 1) * chunk, :], right, preferred_element_type=F32
            )
            grads[c * chunk : (c + 1) * chunk, :] = block
            for t in range(hidden // LANES):
                lanes = jnp.abs(block[:, t * LANES : (t + 1) * LANES]).reshape(-1, 8, LANES)
                highest = jnp.maximum(highest, jnp.max(lanes, axis=0))
        power = power_of(top_of(highest))
        factor = jnp.exp2(-power)
        for owner, (slot, part) in enumerate(SLOTS):
            for t in range(hidden // LANES):
                to = (part * 2 + side) * size + t * row_piece
                out[slot, to : to + row_piece, :] = (
                    grads[
                        owner * row_piece : (owner + 1) * row_piece,
                        t * LANES : (t + 1) * LANES,
                    ]
                    * factor
                )
        powers.append(power)

    outer(1, turned, active[...])
    back = jnp.dot(delta[...], weights[...], preferred_element_type=F32)
    outer(0, normed[...].T, (back * slope[...]).astype(BF16))
    line = lax.broadcasted_iota(jnp.int32, (16, LANES), 0)
    tail = jnp.where(line < 8, powers[1], powers[0])
    for d in range(out.shape[0]):
        out[d, 4 * size :, :] = tail


def collect_kernel(place, came, own, away):
    sources = came.shape[0]
    size = (came.shape[1] - 16) // 4
    for side in range(2):
        factors = [
            jnp.exp2(came[i, 4 * size + 8 * side : 4 * size + 8 * side + 1, 0:1])
            for i in range(sources)
        ]
        for out, core in ((own, place[0]), (away, 1 - place[0])):
            at = pl.multiple_of((core * 2 + side) * size, 8)
            total = came[0, pl.ds(at, size), :] * factors[0]
            for i in range(1, sources):
                total = total + came[i, pl.ds(at, size), :] * factors[i]
            out[side * size : (side + 1) * size, :] = total


def place_kernel(place, own, came, *outs):
    rows = outs[0].shape[0]
    tiles = outs[0].shape[2] // LANES

    def run(sources):
        for out, ref in zip(outs, sources):
            for side in range(2):
                for t in range(tiles):
                    at = (side * tiles + t) * rows
                    out[:, side, t * LANES : (t + 1) * LANES] = ref[at : at + rows, :]

    pl.when(place[0] == 0)(lambda: run((own, came)))
    pl.when(place[0] != 0)(lambda: run((came, own)))


def local(
    latent_noise,
    score_noise,
    timesteps,
    classes,
    class_table,
    gen_weights,
    real_weights,
    fake_weights,
):
    group_index = lax.axis_index("group")
    core = group_index % 2
    y_lo = group_index // 2
    n_dp = lax.axis_size("dp")
    n_mp = lax.axis_size("mp")
    samples, positions, width = latent_noise.shape
    rows = positions // 2
    piece = rows // n_mp
    row_piece, _, hidden = gen_weights.shape
    loss_scale = 1.0 / math.sqrt(samples * n_dp * positions)
    place = jnp.stack([core, y_lo, lax.axis_index("mp")]).astype(jnp.int32)
    work = 2 * rows * width * hidden

    def outgoing(models):
        lanes = hidden * len(models)
        blocks = [shape((4 * n_dp, row_piece, lanes), BF16)]
        return call(lay_kernel, "lay", models, [], blocks)[0]

    def gather(blocks):
        return lax.all_to_all(blocks, PLANE, 0, 0, tiled=True).reshape(width, -1)

    own_class = lax.dynamic_index_in_dim(classes, y_lo, keepdims=False)
    embedding = lax.dynamic_index_in_dim(class_table, own_class, keepdims=True).astype(F32)
    own_step = lax.dynamic_index_in_dim(timesteps, y_lo, keepdims=False)
    phase_angle = 0.5 * jnp.pi / TSTEPS * own_step.astype(F32)
    scales = jnp.stack([jnp.cos(phase_angle), jnp.sin(phase_angle)])
    prepared = call(
        lambda *refs: prepare_kernel(*refs, piece=piece),
        "prepare",
        [latent_noise, score_noise, embedding],
        [place, scales],
        [
            shape((positions, width), BF16),
            shape((2 * piece, width), F32),
            shape((2 * piece, width), F32),
        ],
    )

    gen_mine, score_blocks, prepared, embedding, scales = lax.optimization_barrier(
        (
            gather(outgoing([gen_weights])),
            outgoing([fake_weights, real_weights]),
            prepared,
            embedding,
            scales,
        )
    )
    normed_gen, stream, scaled_noise = prepared
    score_weights = gather(score_blocks)
    gen_other = core_swap(gen_mine)

    steps = n_mp // 2 - 1
    one = shape((piece, width), BF16)
    two = shape((2 * piece, width), BF16)
    preact_gen, active_gen, own, across, *sent = call(
        gen_kernel,
        "generate",
        [normed_gen, gen_mine, gen_other],
        [place],
        [shape((rows, hidden), F32), shape((rows, hidden), BF16), one, one] + [two] * steps,
        2 * work,
        [pltpu.VMEM((rows, width), BF16)],
        room=60,
    )
    came = [paired(block, k + 1) for k, block in enumerate(sent)]
    across = paired(across, n_mp // 2)
    both_f32 = shape((2 * piece, width), F32)
    (sums,) = call(sums_kernel, "sums", [own, across] + came, [place], [both_f32])
    latents, noised, noised_mine = call(
        latent_kernel,
        "latent",
        [sums, core_swap(sums), stream, scaled_noise],
        [place, scales],
        [both_f32, two, one],
    )
    around = [paired(noised, k + 1) for k in range(steps)]
    around.append(paired(noised_mine, n_mp // 2))
    around, later = call(
        order_kernel, "order", around, [], [shape(((2 * steps + 1) * piece, width), BF16)] * 2
    )
    around_other = core_swap(around)
    score_weights, around_other = lax.optimization_barrier((score_weights, around_other))
    (score_parts,) = call(
        score_kernel,
        "score",
        [noised, around, around_other, embedding, score_weights],
        [place],
        [shape((n_mp, 2 * piece, width + LANES), F32)],
        8 * work,
        [pltpu.VMEM((2 * positions, width), BF16)],
    )

    def exchange(blocks):
        return lax.all_to_all(blocks.astype(jnp.float16), "mp", 0, 0, tiled=True).astype(F32)

    (total,) = call(
        total_kernel, "total", [exchange(score_parts)], [], [shape((2 * piece, width), F32)]
    )
    (message,) = call(
        lambda *refs: pack_kernel(*refs, loss_scale=loss_scale),
        "pack",
        [total, core_swap(total), latents, noised],
        [place],
        [shape((2 * piece, width + LANES), F32)],
    )

    message, later = lax.optimization_barrier((message, later))
    normed, preact, active = call(
        refresh_kernel,
        "refresh",
        [noised, later, core_swap(later), embedding, score_weights, normed_gen]
        + [active_gen, core_swap(active_gen), preact_gen, core_swap(preact_gen)],
        [place],
        [
            shape((positions, width), BF16),
            shape((positions, hidden), F32),
            shape((positions, hidden), BF16),
        ],
        2 * work,
    )
    slope = jax.vjp(jax.nn.gelu, preact)[1](jnp.ones_like(preact))[0]
    size = row_piece * hidden // LANES
    (grads,) = call(
        lambda *refs: grad_kernel(
            *refs, loss_scale=loss_scale, count=positions * width, row_piece=row_piece
        ),
        "grads",
        [
            exchange(jnp.broadcast_to(message[None], (n_mp,) + message.shape)),
            jnp.where(core == 0, score_weights[:, hidden:], gen_mine),
            slope,
            normed,
            active,
        ],
        [place],
        [shape((len(WALK), 4 * size + 16, LANES), F32)],
        6 * work,
        [pltpu.VMEM((positions, width), BF16), pltpu.VMEM((width, hidden), F32)],
    )
    came = lax.all_to_all(
        grads.astype(jnp.float16), PLANE, 0, 0, axis_index_groups=PEERS, tiled=True
    )
    own, away = call(
        collect_kernel,
        "collect",
        [came.astype(F32)],
        [place],
        [shape((2 * size, LANES), F32)] * 2,
    )
    fake_grad, gen_grad = call(
        place_kernel,
        "place",
        [own, core_swap(away)],
        [place],
        [shape((row_piece, 2, hidden), F32)] * 2,
    )
    return (gen_grad, fake_grad)


def solution(mesh):
    return jax.shard_map(
        local,
        mesh=mesh,
        in_specs=(
            P("dp", None, None),
            P("dp", None, None),
            P("dp"),
            P("dp"),
            P(),
            P(("group", "dp"), None, "mp"),
            P(("group", "dp"), None, "mp"),
            P(("group", "dp"), None, "mp"),
        ),
        out_specs=(P(("group", "dp"), None, "mp"), P(("group", "dp"), None, "mp")),
        check_vma=False,
    )
```
